32 devices in a mesh: tile: 16 (over z, x, core), chan: 2 (over y).
Axes of the slice: x: 2, y: 2, z: 4, core: 2. Of those that a mesh axis runs over, the one named last changes fastest.
Arguments:
- inputs: bfloat16 [32, 64, 4096], P('tile', 'chan'), may hold values from -6 to 6
- gluing: int32 [32, 4, 3], P('tile'), may hold values from 0 to 31, as said below
- conv_weight: bfloat16 [64, 64, 3, 3], replicated, may hold values from -0.25 to 0.25
- level_weight: bfloat16 [128, 64, 2, 2], replicated, may hold values from -0.375 to 0.375
- cotangent: bfloat16 [32, 128, 1024], P('tile', 'chan'), may hold values from -6 to 6
Outputs:
- level: bfloat16 [32, 128, 1024], P('tile', 'chan')
- grad_inputs: bfloat16 [32, 64, 4096], P('tile', 'chan')
- grad_conv: float32 [64, 64, 3, 3], P(None, 'chan')
- grad_level: float32 [128, 64, 2, 2], P(None, 'chan')
The draws below stay inside these ranges and needn't reach their ends.
Inputs may be any that keep to these rules, and one draw needn't show every extreme that they name: Entry [t, s] = (u, r, f) with r in 0..3 and f in 0..1 says that side s of tile t is glued to side r of tile u; the gluing is symmetric: entry [u, r] is (t, s, f), and no side is glued to itself.
All inputs are finite; a program needn't handle non-finite values.
Results may differ from the reference program's by a relative error of at most 0.005.
Values may be sent and summed in bfloat16 or wider, within the bound.
A program may use at most 128 MiB of HBM per device.

```python
import jax
import jax.numpy as jnp
from jax import lax

C = 64
CO = 128
S = 64
TILES = 32


def draw_gluing(key, part):
    edge_count = 4 * TILES
    order = jax.random.permutation(key, edge_count).astype(jnp.int32)
    first = order[0::2]
    second = order[1::2]
    flips = jax.random.randint(jax.random.fold_in(key, 7), (edge_count // 2,), 0, 2).astype(jnp.int32)
    partner = jnp.zeros((edge_count,), jnp.int32).at[first].set(second).at[second].set(first)
    flipped = jnp.zeros((edge_count,), jnp.int32).at[first].set(flips).at[second].set(flips)
    stacked = jnp.stack([partner // 4, partner % 4, flipped], axis=-1)
    return stacked.reshape(TILES, 4, 3).astype(jnp.int32)


def levels(stream_key, shape, cuts, low, high):
    loudness, own = 1.0, jax.random.fold_in(stream_key, 6)
    for position, parts in cuts:
        heights = jnp.exp(jax.random.uniform(jax.random.fold_in(own, position), (parts,), jnp.float32, low / len(cuts), high / len(cuts)))
        loudness = loudness * jnp.repeat(heights, shape[position] // parts).reshape([-1 if axis == position else 1 for axis in range(len(shape))])
    return loudness


def gaussian(rng, shape, scale, bound, shards=(), kind=jnp.bfloat16):
    drawn = scale * jax.random.normal(rng, shape, jnp.float32)
    if shards:
        drawn = drawn * levels(rng, shape, shards, -0.22, 0.18)
    return jnp.clip(drawn, -bound, bound).astype(kind)


def setup_inputs(seed: int = 0) -> dict:
    key_list = jax.random.split(jax.random.key(seed), 6)
    inputs = gaussian(key_list[0], (TILES, C, S * S), 1.0, 6.0, ((0, 16), (1, 2)))
    gluing = draw_gluing(jax.random.fold_in(key_list[5], 71), 0)
    conv_weight = gaussian(key_list[2], (C, C, 3, 3), (9 * C) ** -0.5, 0.25)
    level_weight = gaussian(key_list[3], (CO, C, 2, 2), (4 * C) ** -0.5, 0.375)
    cotangent = gaussian(key_list[4], (TILES, CO, (S // 2) * (S // 2)), 1.0, 6.0, ((0, 16), (1, 2)))
    return {"inputs": inputs, "gluing": gluing, "conv_weight": conv_weight, "level_weight": level_weight, "cotangent": cotangent}


def edge_strips(source):
    return jnp.stack([source[:, :, 0, :], source[:, :, -1, :], source[:, :, :, 0], source[:, :, :, -1]], axis=1)

def border_strips(padded):
    return jnp.stack([padded[:, :, 0, 1:-1], padded[:, :, -1, 1:-1], padded[:, :, 1:-1, 0], padded[:, :, 1:-1, -1]], axis=1)

def orient(strips, gluing):
    return jnp.where(gluing[:, :, 2][:, :, None, None] == 1, strips[..., ::-1], strips)

def assemble(source, halo_cells):
    tile_count, chan_count = (source.shape[0], source.shape[1])
    corner = jnp.zeros((tile_count, chan_count, 1), source.dtype)
    top_row = jnp.concatenate([corner, halo_cells[:, 0], corner], axis=2)[:, :, None, :]
    low_row = jnp.concatenate([corner, halo_cells[:, 1], corner], axis=2)[:, :, None, :]
    middle = jnp.concatenate([halo_cells[:, 2][:, :, :, None], source, halo_cells[:, 3][:, :, :, None]], axis=3)
    return jnp.concatenate([top_row, middle, low_row], axis=2)

def conv_three(padded, weight):
    extent = padded.shape[2] - 2
    summed = None
    for row_tap in range(3):
        for col_tap in range(3):
            product_term = jnp.einsum('oc,ncxy->noxy', weight[:, :, row_tap, col_tap], padded[:, :, row_tap:row_tap + extent, col_tap:col_tap + extent], preferred_element_type=jnp.float32)
            summed = product_term if summed is None else summed + product_term
    return summed

def conv_two(hidden, weight):
    tile_count, chan_count, extent = (hidden.shape[0], hidden.shape[1], hidden.shape[2])
    summed = None
    for row_tap in range(2):
        for col_tap in range(2):
            sampled = hidden[:, :, row_tap::2, col_tap::2].reshape(tile_count, chan_count, -1)
            product_term = jnp.einsum('oc,ncp->nop', weight[:, :, row_tap, col_tap], sampled, preferred_element_type=jnp.float32)
            summed = product_term if summed is None else summed + product_term
    return summed.reshape(tile_count, weight.shape[0], extent // 2, extent // 2)

def level_grads(hidden, cot_full, weight):
    tile_count, chan_count, extent = (hidden.shape[0], hidden.shape[1], hidden.shape[2])
    half = extent // 2
    cot_rows = cot_full.reshape(tile_count, cot_full.shape[1], -1)
    weight_rows = []
    spread_rows = []
    for row_tap in range(2):
        weight_cols = []
        spread_cols = []
        for col_tap in range(2):
            sampled = hidden[:, :, row_tap::2, col_tap::2].reshape(tile_count, chan_count, -1)
            weight_cols.append(jnp.einsum('nop,ncp->oc', cot_rows, sampled, preferred_element_type=jnp.float32))
            spread = jnp.einsum('oc,nop->ncp', weight[:, :, row_tap, col_tap], cot_rows, preferred_element_type=jnp.float32)
            spread_cols.append(spread.reshape(tile_count, chan_count, half, half))
        weight_rows.append(jnp.stack(weight_cols, axis=-1))
        spread_rows.append(jnp.stack(spread_cols, axis=-1))
    grad_weight = jnp.stack(weight_rows, axis=2)
    grad_hidden = jnp.stack(spread_rows, axis=3).reshape(tile_count, chan_count, extent, extent)
    return (grad_weight, grad_hidden)

def conv_grads(padded, grad_full, weight):
    extent = padded.shape[2] - 2
    grad_padded = jnp.zeros(padded.shape, jnp.float32)
    weight_rows = []
    for row_tap in range(3):
        weight_cols = []
        for col_tap in range(3):
            window = padded[:, :, row_tap:row_tap + extent, col_tap:col_tap + extent]
            weight_cols.append(jnp.einsum('noxy,ncxy->oc', grad_full, window, preferred_element_type=jnp.float32))
            spread = jnp.einsum('oc,noxy->ncxy', weight[:, :, row_tap, col_tap], grad_full, preferred_element_type=jnp.float32)
            grad_padded = grad_padded.at[:, :, row_tap:row_tap + extent, col_tap:col_tap + extent].add(spread)
        weight_rows.append(jnp.stack(weight_cols, axis=-1))
    return (jnp.stack(weight_rows, axis=2), grad_padded)

def reference(inputs, gluing, conv_weight, level_weight, cotangent):
    tile_count = inputs.shape[0]
    inputs = inputs.reshape(tile_count, inputs.shape[1], S, S)
    cotangent = cotangent.reshape(tile_count, cotangent.shape[1], S // 2, S // 2)
    target = (gluing[:, :, 0] * 4 + gluing[:, :, 1]).reshape(-1).astype(jnp.int32)

    def route(strips):
        rows_flat = strips.reshape((tile_count * 4,) + strips.shape[2:])
        chosen = jnp.take(rows_flat, target, axis=0).reshape(strips.shape)
        return orient(chosen, gluing)
    padded = assemble(inputs, route(edge_strips(inputs)))
    conv_float = conv_weight.astype(jnp.float32)
    level_float = level_weight.astype(jnp.float32)

    def per_tile(pair):
        padded_tile = pair[0][None].astype(jnp.float32)
        cot_tile = pair[1][None].astype(jnp.float32)
        pre_act = conv_three(padded_tile, conv_float)
        hidden = jax.nn.gelu(pre_act).astype(jnp.bfloat16)
        level = conv_two(hidden.astype(jnp.float32), level_float).astype(jnp.bfloat16)
        grad_level, grad_hidden = level_grads(hidden.astype(jnp.float32), cot_tile, level_float)
        unused, pullback = jax.vjp(jax.nn.gelu, pre_act)
        grad_pre = pullback(grad_hidden)[0].astype(jnp.bfloat16)
        grad_conv, grad_padded = conv_grads(padded_tile, grad_pre.astype(jnp.float32), conv_float)
        rims = border_strips(grad_padded).astype(jnp.bfloat16)
        return (level[0], grad_conv, grad_level, rims[0], grad_padded[0, :, 1:-1, 1:-1])
    level, conv_terms, level_terms, rims, interior = lax.map(per_tile, (padded, cotangent))
    returned = route(rims).astype(jnp.float32)
    interior = interior.at[:, :, 0, :].add(returned[:, 0])
    interior = interior.at[:, :, -1, :].add(returned[:, 1])
    interior = interior.at[:, :, :, 0].add(returned[:, 2])
    interior = interior.at[:, :, :, -1].add(returned[:, 3])
    grad_conv = lax.optimization_barrier(jnp.sum(conv_terms, axis=0))
    grad_level = lax.optimization_barrier(jnp.sum(level_terms, axis=0))
    level = level.reshape(tile_count, level.shape[1], -1)
    grad_inputs = interior.astype(jnp.bfloat16).reshape(tile_count, interior.shape[1], -1)
    return (level, grad_inputs, grad_conv, grad_level)
```

```python
import functools

import jax
import jax.numpy as jnp
import numpy as np
from jax import lax
from jax.experimental import pallas as pl
from jax.experimental.pallas import tpu as pltpu
from jax.sharding import PartitionSpec as P

S = 64


def edge_strips(source):
    return jnp.stack(
        [source[:, :, 0, :], source[:, :, -1, :], source[:, :, :, 0], source[:, :, :, -1]], axis=1
    )


def border_strips(padded):
    return jnp.stack(
        [
            padded[:, :, 0, 1:-1],
            padded[:, :, -1, 1:-1],
            padded[:, :, 1:-1, 0],
            padded[:, :, 1:-1, -1],
        ],
        axis=1,
    )


def orient(strips, gluing):
    return jnp.where(gluing[:, :, 2][:, :, None, None] == 1, strips[..., ::-1], strips)


def make_picker(gluing):
    target = gluing[:, :, 0] * 4 + gluing[:, :, 1]

    def picker(current, received, first_row):
        strip_count = received.shape[0] * 4
        received_rows = received.reshape((strip_count,) + received.shape[2:])
        inside = (target >= 0) & (target < strip_count)
        chosen = jnp.take(received_rows, jnp.clip(target, 0, strip_count - 1), axis=0)
        return jnp.where(inside[:, :, None, None], chosen, current)

    return picker


def assemble(source, halo_cells):
    tile_count, chan_count = (source.shape[0], source.shape[1])
    corner = jnp.zeros((tile_count, chan_count, 1), source.dtype)
    top_row = jnp.concatenate([corner, halo_cells[:, 0], corner], axis=2)[:, :, None, :]
    low_row = jnp.concatenate([corner, halo_cells[:, 1], corner], axis=2)[:, :, None, :]
    middle = jnp.concatenate(
        [halo_cells[:, 2][:, :, :, None], source, halo_cells[:, 3][:, :, :, None]], axis=3
    )
    return jnp.concatenate([top_row, middle, low_row], axis=2)


def conv_three(padded, weight):
    extent = padded.shape[2] - 2
    summed = None
    for row_tap in range(3):
        for col_tap in range(3):
            product_term = jnp.einsum(
                "oc,ncxy->noxy",
                weight[:, :, row_tap, col_tap],
                padded[:, :, row_tap : row_tap + extent, col_tap : col_tap + extent],
                preferred_element_type=jnp.float32,
            )
            summed = product_term if summed is None else summed + product_term
    return summed


def conv_two(hidden, weight):
    tile_count, chan_count, extent = (hidden.shape[0], hidden.shape[1], hidden.shape[2])
    summed = None
    for row_tap in range(2):
        for col_tap in range(2):
            sampled = hidden[:, :, row_tap::2, col_tap::2].reshape(tile_count, chan_count, -1)
            product_term = jnp.einsum(
                "oc,ncp->nop",
                weight[:, :, row_tap, col_tap],
                sampled,
                preferred_element_type=jnp.float32,
            )
            summed = product_term if summed is None else summed + product_term
    return summed.reshape(tile_count, weight.shape[0], extent // 2, extent // 2)


def level_grads(hidden, cot_full, weight):
    tile_count, chan_count, extent = (hidden.shape[0], hidden.shape[1], hidden.shape[2])
    half = extent // 2
    cot_rows = cot_full.reshape(tile_count, cot_full.shape[1], -1)
    weight_rows = []
    spread_rows = []
    for row_tap in range(2):
        weight_cols = []
        spread_cols = []
        for col_tap in range(2):
            sampled = hidden[:, :, row_tap::2, col_tap::2].reshape(tile_count, chan_count, -1)
            weight_cols.append(
                jnp.einsum("nop,ncp->oc", cot_rows, sampled, preferred_element_type=jnp.float32)
            )
            spread = jnp.einsum(
                "oc,nop->ncp",
                weight[:, :, row_tap, col_tap],
                cot_rows,
                preferred_element_type=jnp.float32,
            )
            spread_cols.append(spread.reshape(tile_count, chan_count, half, half))
        weight_rows.append(jnp.stack(weight_cols, axis=-1))
        spread_rows.append(jnp.stack(spread_cols, axis=-1))
    grad_weight = jnp.stack(weight_rows, axis=2)
    grad_hidden = jnp.stack(spread_rows, axis=3).reshape(tile_count, chan_count, extent, extent)
    return (grad_weight, grad_hidden)


def conv_grads(padded, grad_full, weight):
    extent = padded.shape[2] - 2
    grad_padded = jnp.zeros(padded.shape, jnp.float32)
    weight_rows = []
    for row_tap in range(3):
        weight_cols = []
        for col_tap in range(3):
            window = padded[:, :, row_tap : row_tap + extent, col_tap : col_tap + extent]
            weight_cols.append(
                jnp.einsum("noxy,ncxy->oc", grad_full, window, preferred_element_type=jnp.float32)
            )
            spread = jnp.einsum(
                "oc,noxy->ncxy",
                weight[:, :, row_tap, col_tap],
                grad_full,
                preferred_element_type=jnp.float32,
            )
            grad_padded = grad_padded.at[
                :, :, row_tap : row_tap + extent, col_tap : col_tap + extent
            ].add(spread)
        weight_rows.append(jnp.stack(weight_cols, axis=-1))
    return (jnp.stack(weight_rows, axis=2), grad_padded)


def add_returned(grad_padded, returned):
    interior = grad_padded[:, :, 1:-1, 1:-1]
    interior = interior.at[:, :, 0, :].add(returned[:, 0])
    interior = interior.at[:, :, -1, :].add(returned[:, 1])
    interior = interior.at[:, :, :, 0].add(returned[:, 2])
    interior = interior.at[:, :, :, -1].add(returned[:, 3])
    return interior.astype(jnp.bfloat16)


def flatten_pixels(field):
    return field.reshape(field.shape[0], field.shape[1], -1)


def on_device_general(inputs, gluing, conv_weight, level_weight, cotangent):
    inputs = inputs.reshape(inputs.shape[0], inputs.shape[1], S, S)
    cotangent = cotangent.reshape(cotangent.shape[0], cotangent.shape[1], S // 2, S // 2)
    chan_width = inputs.shape[1]
    chan_first = lax.axis_index("chan") * chan_width
    tile_share = inputs.shape[0] // lax.axis_size("chan")
    tile_first = lax.axis_index("chan") * tile_share
    local_gluing = lax.dynamic_slice_in_dim(gluing, tile_first, tile_share, 0)
    picker = make_picker(local_gluing)
    whole_input, cot_full = (
        lax.all_to_all(inputs, "chan", split_axis=0, concat_axis=1, tiled=True),
        lax.all_to_all(cotangent, "chan", split_axis=0, concat_axis=1, tiled=True),
    )
    strips = edge_strips(whole_input)
    halo_cells = picker(
        jnp.zeros_like(strips),
        lax.all_gather(strips, ("tile", "chan"), axis=0, tiled=True),
        jnp.int32(0),
    )
    padded_whole = assemble(whole_input, orient(halo_cells, local_gluing))
    pre_act = conv_three(padded_whole, conv_weight)
    hidden = jax.nn.gelu(pre_act).astype(jnp.bfloat16)
    level_whole = conv_two(hidden, level_weight).astype(jnp.bfloat16)
    level = lax.all_to_all(level_whole, "chan", split_axis=1, concat_axis=0, tiled=True)
    grad_level, grad_hidden = level_grads(hidden, cot_full, level_weight)
    unused, pullback = jax.vjp(jax.nn.gelu, pre_act)
    grad_pre = pullback(grad_hidden)[0].astype(jnp.bfloat16)
    grad_conv, grad_padded = conv_grads(padded_whole, grad_pre, conv_weight)
    grad_conv, grad_level = lax.psum((grad_conv, grad_level), ("tile", "chan"))
    grad_conv = lax.dynamic_slice_in_dim(grad_conv, chan_first, chan_width, 1)
    grad_level = lax.dynamic_slice_in_dim(grad_level, chan_first, chan_width, 1)
    rims = border_strips(grad_padded).astype(jnp.bfloat16)
    returned = picker(
        jnp.zeros_like(rims),
        lax.all_gather(rims, ("tile", "chan"), axis=0, tiled=True),
        jnp.int32(0),
    )
    returned = orient(returned, local_gluing).astype(jnp.float32)
    grad_whole = add_returned(grad_padded, returned)
    grad_inputs = lax.all_to_all(grad_whole, "chan", split_axis=1, concat_axis=0, tiled=True)
    return (flatten_pixels(level), flatten_pixels(grad_inputs), grad_conv, grad_level)


MESH = pl.DeviceIdType.MESH
F32 = jnp.float32
BF16 = jnp.bfloat16
PIX = 1024
HALF = 32
ROOT = 0.7978845608028654
CUBIC = 0.044715


def split_matrix():
    lane = np.arange(512)
    row, col = lane // 64, lane % 64
    out = ((row % 2) * 2 + col % 2) * 128 + (row // 2) * 32 + col // 2
    matrix = np.zeros((512, 512), np.float32)
    matrix[lane, out] = 1.0
    return matrix


def spread_matrices():
    rows = np.zeros((128, PIX), np.float32)
    cols = np.zeros((128, PIX), np.float32)
    index = np.arange(HALF)
    rows[index, index] = 1.0
    rows[32 + index, 31 * HALF + index] = 1.0
    cols[64 + index, index * HALF] = 1.0
    cols[96 + index, index * HALF + 31] = 1.0
    return rows, cols


def strip_matrix():
    index = np.arange(64)
    slot = (index % 2) * 32 + index // 2
    matrix = np.zeros((4096, 256), np.float32)
    matrix[index, slot] = 1.0
    matrix[63 * 64 + index, 64 + slot] = 1.0
    matrix[index * 64, 128 + slot] = 1.0
    matrix[index * 64 + 63, 192 + slot] = 1.0
    return matrix


def dot(left, right):
    return jnp.dot(left, right, preferred_element_type=F32)


def dot_last(left, right):
    return lax.dot_general(left, right, (((1,), (1,)), ((), ())), preferred_element_type=F32)


def reverse_matrix():
    row = lax.broadcasted_iota(jnp.int32, (128, 128), 0)
    col = lax.broadcasted_iota(jnp.int32, (128, 128), 1)
    same = (row // 64) == (col // 64)
    return (same & ((row % 64) + (col % 64) == 63)).astype(F32).astype(BF16)


def route(codes, strips, source):
    strips = strips.astype(BF16)
    straight = (codes == 2 * source).astype(F32).astype(BF16)
    turned = (codes == 2 * source + 1).astype(F32).astype(BF16)
    reverse = dot(strips, reverse_matrix()).astype(BF16)
    return dot(straight, strips) + dot(turned, reverse)


def greet_all(me):
    barrier = pltpu.get_barrier_semaphore()

    def greet(step, carry):
        other = lax.rem(me + step, 32)
        pl.semaphore_signal(
            barrier, inc=1, device_id=(other // 2, lax.rem(other, 2)), device_id_type=MESH
        )
        return carry

    lax.fori_loop(1, 32, greet, 0)
    pl.semaphore_wait(barrier, 31)


def remote(src, dst, send, recv, tile, chan):
    return pltpu.make_async_remote_copy(
        src_ref=src, dst_ref=dst, send_sem=send, recv_sem=recv,
        device_id=(tile, chan), device_id_type=MESH,
    )


def loop(first, last, body):
    def step(index, carry):
        body(index)
        return carry

    lax.fori_loop(first, last, step, 0)


def gather_kernel(
    x_ref, cot_ref, strips_ref, codes_ref,
    xo_ref, co_ref, halo_ref, all_ref,
    held, routed,
    big_send, big_recv, one_send, one_recv, code_send, code_recv, two_send, two_recv,
):
    row, half = lax.axis_index("tile"), lax.axis_index("chan")
    me = row * 2 + half
    other = 1 - half
    greet_all(me)

    def to_row(step):
        j = lax.rem(row + step, 16)
        yield remote(codes_ref, all_ref.at[row], code_send.at[j], code_recv.at[row], j, half)
        yield remote(strips_ref.at[j], held.at[row], one_send.at[j], one_recv.at[row], j, half)

    def from_row(step):
        j = lax.rem(row + step, 16)
        yield remote(codes_ref, all_ref.at[j], code_send.at[j], code_recv.at[j], j, half)
        yield remote(strips_ref.at[j], held.at[j], one_send.at[j], one_recv.at[j], j, half)

    loop(1, 16, lambda step: [copy.start() for copy in to_row(step)])
    x_copy = remote(x_ref.at[other], xo_ref.at[half], big_send.at[0], big_recv.at[0], row, other)
    c_copy = remote(cot_ref.at[other], co_ref.at[half], big_send.at[1], big_recv.at[1], row, other)
    x_copy.start()
    c_copy.start()
    held[row] = strips_ref[row]
    all_ref[row] = codes_ref[...]
    xo_ref[half] = x_ref[half]
    co_ref[half] = cot_ref[half]
    loop(1, 16, lambda step: [copy.wait_recv() for copy in from_row(step)])
    lane = lax.broadcasted_iota(jnp.int32, (128, 128), 1)
    answer = route(all_ref[...].reshape(128, 128), held[...].reshape(128, 128), lane)
    routed[...] = answer.reshape(16, 8, 128)

    def to_all(step):
        q = lax.rem(me + step, 32)
        return remote(
            routed.at[q // 2], halo_ref.at[me], two_send.at[q], two_recv.at[me], q // 2, lax.rem(q, 2)
        )

    def from_all(step):
        q = lax.rem(me + step, 32)
        return remote(
            routed.at[q // 2], halo_ref.at[q], two_send.at[q], two_recv.at[q], q // 2, lax.rem(q, 2)
        )

    loop(1, 32, lambda step: to_all(step).start())
    halo_ref[me] = routed[row]
    loop(1, 32, lambda step: from_all(step).wait_recv())
    x_copy.wait()
    c_copy.wait()
    loop(1, 16, lambda step: [copy.wait_send() for copy in to_row(step)])
    loop(1, 32, lambda step: to_all(step).wait_send())


def masks():
    pixel = lax.broadcasted_iota(jnp.int32, (64, PIX), 1)
    return pixel < 32, pixel >= 992, (pixel % 32) == 0, (pixel % 32) == 31


def patches(planes, rows, cols, out_ref):
    top, low, left, right = masks()
    zero = jnp.zeros((64, PIX), F32)

    def ahead(value, by):
        return pltpu.roll(value, by % PIX, 1)

    def column(a, s):
        if s in (0, 1):
            return planes[a][s]
        beside = zero if cols is None else cols[a]
        if s < 0:
            return jnp.where(left, beside, ahead(planes[a][1], 1))
        return jnp.where(right, beside, ahead(planes[a][0], -1))

    def outer(s):
        if rows is None:
            return zero
        if s in (0, 1):
            return rows[s]
        if s < 0:
            return jnp.where(left, 0.0, ahead(rows[1], 1))
        return jnp.where(right, 0.0, ahead(rows[0], -1))

    for s in range(-1, 3):
        even, odd = column(0, s), column(1, s)
        edge = outer(s)
        parts = (
            jnp.where(top, edge, ahead(odd, 32)), even, odd, jnp.where(low, edge, ahead(even, -32))
        )
        for r in range(4):
            first = (r * 4 + s + 1) * 64
            out_ref[first:first + 64, :] = parts[r].astype(BF16)


def work_kernel(
    x_ref, cot_ref, halo_ref, wide_ref, back_ref, turn_ref, lw_ref, lwt_ref, split_ref, rows_ref, cols_ref,
    level_ref, gi_ref, rims_ref, gc_ref, gl_ref,
    z_ref, zg_ref,
):
    x = x_ref[...]
    stacked = jnp.concatenate([x[:, 512 * k:512 * k + 512] for k in range(8)], axis=0)
    split = dot(stacked, split_ref[...])

    def plane(index):
        return jnp.concatenate(
            [split[64 * k:64 * k + 64, 128 * index:128 * index + 128] for k in range(8)], axis=1
        )

    halo = halo_ref[...]
    rows = dot(halo, rows_ref[...])
    cols = dot(halo, cols_ref[...])
    patches(
        [[plane(0), plane(1)], [plane(2), plane(3)]],
        [rows[:64], rows[64:]], [cols[:64], cols[64:]], z_ref,
    )
    pre = dot(wide_ref[...], z_ref[...])
    square = pre * pre
    bent = jnp.tanh(ROOT * pre * (1.0 + CUBIC * square))
    hidden = (0.5 * pre * (1.0 + bent)).astype(BF16)
    slope = 0.5 * (1.0 + bent) + 0.5 * pre * (1.0 - bent * bent) * ROOT * (1.0 + 3.0 * CUBIC * square)
    level_ref[...] = dot(lw_ref[...], hidden).astype(BF16)
    cot = cot_ref[...]
    gl_ref[...] = dot_last(cot, hidden)
    grad_pre = (dot(lwt_ref[...], cot) * slope).astype(BF16)
    wide_grad = dot_last(grad_pre, z_ref[...])
    for i in range(3):
        for j in range(3):
            total = None
            for a in range(2):
                for b in range(2):
                    first, at = (a * 2 + b) * 64, ((a + i) * 4 + b + j) * 64
                    term = wide_grad[first:first + 64, at:at + 64]
                    total = term if total is None else total + term
            gc_ref[i * 3 + j] = total
    wide = grad_pre.astype(F32)
    patches(
        [[wide[0:64], wide[64:128]], [wide[128:192], wide[192:256]]], None, None, zg_ref
    )
    gi_ref[...] = dot(back_ref[...], zg_ref[...])
    edge = dot_last(grad_pre, rows_ref[...] + cols_ref[...]).astype(BF16)
    spill = dot(turn_ref[...], edge)
    lane = lax.broadcasted_iota(jnp.int32, (64, 128), 1)

    def around(k):
        def block(r, s):
            first = (r * 4 + s) * 64
            return spill[first:first + 64, :]

        low = jnp.where(lane < 32, block(0, k), block(3, k))
        high = jnp.where(lane < 96, block(k, 0), block(k, 3))
        return jnp.where(lane < 64, low, high)

    inner = lane % 32
    before = jnp.where(inner == 0, 0.0, pltpu.roll(around(3), 1, 1))
    after = jnp.where(inner == 31, 0.0, pltpu.roll(around(0), 127, 1))
    rims_ref[:64, :] = (around(1) + before).astype(BF16).astype(F32)
    rims_ref[64:, :] = (around(2) + after).astype(BF16).astype(F32)


def return_kernel(
    level_ref, rims_ref, codes_ref, grads_ref,
    lo_ref, back_ref, sums_ref,
    held, routed, parts, total,
    big_send, big_recv, one_send, one_recv, two_send, two_recv, w_send, w_recv, s_send, s_recv,
):
    row, half = lax.axis_index("tile"), lax.axis_index("chan")
    me = row * 2 + half
    other = 1 - half
    greet_all(me)

    def place(step):
        q = lax.rem(me + step, 32)
        return q, q // 2, lax.rem(q, 2)

    def rim_to(step):
        q, j, c = place(step)
        return remote(rims_ref.at[q], held.at[me], one_send.at[q], one_recv.at[me], j, c)

    def rim_from(step):
        q, j, c = place(step)
        return remote(rims_ref.at[q], held.at[q], one_send.at[q], one_recv.at[q], j, c)

    def grad_to(step):
        q, j, c = place(step)
        return remote(grads_ref.at[q], parts.at[me], w_send.at[q], w_recv.at[me], j, c)

    def grad_from(step):
        q, j, c = place(step)
        return remote(grads_ref.at[q], parts.at[q], w_send.at[q], w_recv.at[q], j, c)

    loop(1, 32, lambda step: rim_to(step).start())
    loop(1, 32, lambda step: grad_to(step).start())
    l_copy = remote(level_ref.at[other], lo_ref.at[half], big_send.at[0], big_recv.at[0], row, other)
    l_copy.start()
    held[me] = rims_ref[me]
    parts[me] = grads_ref[me]
    lo_ref[half] = level_ref[half]
    loop(1, 32, lambda step: rim_from(step).wait_recv())
    lane = lax.broadcasted_iota(jnp.int32, (128, 256), 1)
    codes = codes_ref[...].reshape(128, 128)
    codes = jnp.concatenate([codes, codes], axis=1)
    source = jnp.where((lane % 8) < 4, (lane // 8) * 4 + lane % 8, -1)
    answer = route(codes, held[...].reshape(256, 128), source)
    routed[...] = answer.reshape(16, 8, 128)

    def all_to(step):
        q, j, c = place(step)
        return remote(routed.at[j], back_ref.at[me], two_send.at[q], two_recv.at[me], j, c)

    def all_from(step):
        q, j, c = place(step)
        return remote(routed.at[j], back_ref.at[q], two_send.at[q], two_recv.at[q], j, c)

    loop(1, 32, lambda step: all_to(step).start())
    back_ref[me] = routed[row]
    loop(1, 32, lambda step: grad_from(step).wait_recv())
    total[...] = jnp.sum(parts[...], axis=0)

    def sum_to(step):
        j = lax.rem(row + step, 16)
        return remote(total, sums_ref.at[row], s_send.at[j], s_recv.at[row], j, half)

    def sum_from(step):
        j = lax.rem(row + step, 16)
        return remote(total, sums_ref.at[j], s_send.at[j], s_recv.at[j], j, half)

    loop(1, 16, lambda step: sum_to(step).start())
    sums_ref[row] = total[...]
    loop(1, 32, lambda step: all_from(step).wait_recv())
    loop(1, 16, lambda step: sum_from(step).wait_recv())
    l_copy.wait()
    loop(1, 32, lambda step: rim_to(step).wait_send())
    loop(1, 32, lambda step: grad_to(step).wait_send())
    loop(1, 32, lambda step: all_to(step).wait_send())
    loop(1, 16, lambda step: sum_to(step).wait_send())


def finish_kernel(
    gi_ref, back_ref, rows_ref, cols_ref, split_ref,
    out_ref,
    mine, send_sem, recv_sem,
):
    row, half = lax.axis_index("tile"), lax.axis_index("chan")
    other = 1 - half
    barrier = pltpu.get_barrier_semaphore()
    pl.semaphore_signal(barrier, inc=1, device_id=(row, other), device_id_type=MESH)
    rows = dot(back_ref[...], rows_ref[...])
    cols = dot(back_ref[...], cols_ref[...])
    top, low, left, right = masks()
    planes = []
    for a in range(2):
        for b in range(2):
            first = (a * 2 + b) * 64
            whole = gi_ref[first:first + 64, :]
            whole = whole + jnp.where(low if a else top, rows[b * 64:b * 64 + 64], 0.0)
            whole = whole + jnp.where(right if b else left, cols[a * 64:a * 64 + 64], 0.0)
            planes.append(whole.astype(BF16))
    stacked = jnp.concatenate(
        [
            jnp.concatenate([part[:, 128 * k:128 * k + 128] for part in planes], axis=1)
            for k in range(8)
        ],
        axis=0,
    )
    joined = dot_last(stacked, split_ref[...]).astype(BF16)
    for k in range(8):
        for h in range(2):
            first = 64 * k + 32 * h
            mine[h, :, 512 * k:512 * k + 512] = joined[first:first + 32, :]
    pl.semaphore_wait(barrier, 1)
    copy = remote(mine.at[other], out_ref.at[half], send_sem, recv_sem, row, other)
    copy.start()
    out_ref[half] = mine[half]
    copy.wait()


def vmem(count):
    return [pl.BlockSpec(memory_space=pltpu.VMEM)] * count


def shape(dims, kind):
    return jax.ShapeDtypeStruct(dims, kind)


def params(**extra):
    return pltpu.CompilerParams(vmem_limit_bytes=48 * 1024 * 1024, **extra)


def spread_taps(weight, flip):
    blocks = []
    for a in range(2):
        for b in range(2):
            low, left = a, b
            grown = jnp.pad(
                weight, ((low, 1 - low), (left, 1 - left), (0, 0), (0, 0))
            )
            blocks.append(grown.transpose(2, 0, 1, 3).reshape(64, 1024))
    return jnp.concatenate(blocks, axis=0)


def on_device_fast(inputs, gluing, conv_weight, level_weight, cotangent):
    half = lax.axis_index("chan")
    dma = pltpu.SemaphoreType.DMA
    rows_np, cols_np = spread_matrices()
    rows_mat, cols_mat = jnp.asarray(rows_np, BF16), jnp.asarray(cols_np, BF16)
    split_mat = jnp.asarray(split_matrix(), BF16)
    taps = conv_weight.transpose(2, 3, 0, 1)
    wide = spread_taps(taps, False)
    back = spread_taps(taps[::-1, ::-1].transpose(0, 1, 3, 2), True)
    turn = wide.T
    lw = level_weight.transpose(0, 2, 3, 1).reshape(128, 256)
    lwt = lw.T

    strips = jnp.einsum("tcp,pk->tck", inputs, jnp.asarray(strip_matrix(), BF16), preferred_element_type=F32)
    strips = strips.reshape(2, 16, 2, 4, 64).transpose(1, 0, 3, 2, 4).reshape(16, 8, 128)
    codes = ((gluing[:, :, 0] * 4 + gluing[:, :, 1]) * 2 + gluing[:, :, 2]).reshape(8, 1)
    codes = jnp.broadcast_to(codes, (8, 128))
    whole, cot, halo, all_codes = pl.pallas_call(
        gather_kernel,
        out_shape=(
            shape((2, 32, 4096), BF16), shape((2, 64, 1024), BF16),
            shape((32, 8, 128), F32), shape((16, 8, 128), jnp.int32),
        ),
        in_specs=vmem(4),
        out_specs=tuple(vmem(4)),
        scratch_shapes=[
            pltpu.VMEM((16, 8, 128), F32), pltpu.VMEM((16, 8, 128), F32),
            dma((2,)), dma((2,)), dma((16,)), dma((16,)), dma((16,)), dma((16,)), dma((32,)), dma((32,)),
        ],
        compiler_params=params(collective_id=0, has_side_effects=True),
        name="gather",
    )(inputs, cotangent, strips, codes)

    def unpack(field):
        mine = lax.dynamic_slice_in_dim(field, half * 4, 4, 1)
        mine = mine.reshape(16, 2, 4, 2, 2, 32).transpose(4, 1, 0, 3, 2, 5)
        return mine.reshape(128, 128).astype(BF16)

    level, gi, rims, gc, gl = pl.pallas_call(
        work_kernel,
        out_shape=(
            shape((128, 1024), BF16), shape((256, 1024), F32), shape((128, 128), F32),
            shape((9, 64, 64), F32), shape((128, 256), F32),
        ),
        in_specs=vmem(11),
        out_specs=tuple(vmem(5)),
        scratch_shapes=[pltpu.VMEM((1024, 1024), BF16), pltpu.VMEM((1024, 1024), BF16)],
        compiler_params=params(),
        name="work",
    )(
        whole.reshape(64, 4096), cot.reshape(128, 1024), unpack(halo), wide, back, turn, lw, lwt,
        split_mat, rows_mat, cols_mat,
    )
    rims = rims.reshape(2, 2, 16, 2, 4, 32).transpose(2, 1, 4, 3, 0, 5).reshape(32, 4, 128)
    rims = jnp.pad(rims, ((0, 0), (0, 4), (0, 0)))
    gc = gc.reshape(9, 64, 2, 32).transpose(2, 0, 1, 3).reshape(2, 144, 128)
    gl = gl.reshape(128, 4, 2, 32).transpose(2, 1, 0, 3).reshape(2, 128, 128)
    grads = jnp.concatenate([gc, gl, jnp.zeros((2, 112, 128), F32)], axis=1)
    grads = grads.reshape(2, 16, 24, 128).transpose(1, 0, 2, 3).reshape(32, 24, 128)
    level, returned, sums = pl.pallas_call(
        return_kernel,
        out_shape=(
            shape((2, 64, 1024), BF16), shape((32, 8, 128), F32), shape((16, 24, 128), F32),
        ),
        in_specs=vmem(4),
        out_specs=tuple(vmem(3)),
        scratch_shapes=[
            pltpu.VMEM((32, 8, 128), F32), pltpu.VMEM((16, 8, 128), F32),
            pltpu.VMEM((32, 24, 128), F32), pltpu.VMEM((24, 128), F32),
            dma((1,)), dma((1,)), dma((32,)), dma((32,)), dma((32,)), dma((32,)),
            dma((32,)), dma((32,)), dma((16,)), dma((16,)),
        ],
        compiler_params=params(collective_id=1, has_side_effects=True),
        name="return",
    )(level.reshape(2, 64, 1024), rims, all_codes, grads)
    grad_inputs = pl.pallas_call(
        finish_kernel,
        out_shape=shape((2, 32, 4096), BF16),
        in_specs=vmem(5),
        out_specs=pl.BlockSpec(memory_space=pltpu.VMEM),
        scratch_shapes=[pltpu.VMEM((2, 32, 4096), BF16), dma(()), dma(())],
        compiler_params=params(collective_id=2, has_side_effects=True),
        name="finish",
    )(gi, unpack(returned), rows_mat, cols_mat, split_mat)
    sums = sums.reshape(384, 128)
    grad_conv = sums[:144].reshape(3, 3, 64, 32).transpose(2, 3, 0, 1)
    grad_level = sums[144:272].reshape(2, 2, 128, 32).transpose(2, 3, 0, 1)
    return level, grad_inputs, grad_conv, grad_level


def solution(mesh):
    fits = mesh.shape["tile"] == 16 and mesh.shape["chan"] == 2
    return jax.shard_map(
        on_device_fast if fits else on_device_general,
        mesh=mesh,
        in_specs=(
            P("tile", "chan", None),
            P("tile", None, None),
            P(),
            P(),
            P("tile", "chan", None),
        ),
        out_specs=(
            P("tile", "chan", None),
            P("tile", "chan", None),
            P(None, "chan", None, None),
            P(None, "chan", None, None),
        ),
        check_vma=False,
    )
```

```python
import functools

import jax
import jax.numpy as jnp
import numpy as np
from jax import lax
from jax.experimental import pallas as pl
from jax.experimental.pallas import tpu as pltpu
from jax.sharding import PartitionSpec as P

S = 64


def edge_strips(source):
    return jnp.stack(
        [source[:, :, 0, :], source[:, :, -1, :], source[:, :, :, 0], source[:, :, :, -1]], axis=1
    )


def border_strips(padded):
    return jnp.stack(
        [
            padded[:, :, 0, 1:-1],
            padded[:, :, -1, 1:-1],
            padded[:, :, 1:-1, 0],
            padded[:, :, 1:-1, -1],
        ],
        axis=1,
    )


def orient(strips, gluing):
    return jnp.where(gluing[:, :, 2][:, :, None, None] == 1, strips[..., ::-1], strips)


def make_picker(gluing):
    target = gluing[:, :, 0] * 4 + gluing[:, :, 1]

    def picker(current, received, first_row):
        strip_count = received.shape[0] * 4
        received_rows = received.reshape((strip_count,) + received.shape[2:])
        inside = (target >= 0) & (target < strip_count)
        chosen = jnp.take(received_rows, jnp.clip(target, 0, strip_count - 1), axis=0)
        return jnp.where(inside[:, :, None, None], chosen, current)

    return picker


def assemble(source, halo_cells):
    tile_count, chan_count = (source.shape[0], source.shape[1])
    corner = jnp.zeros((tile_count, chan_count, 1), source.dtype)
    top_row = jnp.concatenate([corner, halo_cells[:, 0], corner], axis=2)[:, :, None, :]
    low_row = jnp.concatenate([corner, halo_cells[:, 1], corner], axis=2)[:, :, None, :]
    middle = jnp.concatenate(
        [halo_cells[:, 2][:, :, :, None], source, halo_cells[:, 3][:, :, :, None]], axis=3
    )
    return jnp.concatenate([top_row, middle, low_row], axis=2)


def conv_three(padded, weight):
    extent = padded.shape[2] - 2
    summed = None
    for row_tap in range(3):
        for col_tap in range(3):
            product_term = jnp.einsum(
                "oc,ncxy->noxy",
                weight[:, :, row_tap, col_tap],
                padded[:, :, row_tap : row_tap + extent, col_tap : col_tap + extent],
                preferred_element_type=jnp.float32,
            )
            summed = product_term if summed is None else summed + product_term
    return summed


def conv_two(hidden, weight):
    tile_count, chan_count, extent = (hidden.shape[0], hidden.shape[1], hidden.shape[2])
    summed = None
    for row_tap in range(2):
        for col_tap in range(2):
            sampled = hidden[:, :, row_tap::2, col_tap::2].reshape(tile_count, chan_count, -1)
            product_term = jnp.einsum(
                "oc,ncp->nop",
                weight[:, :, row_tap, col_tap],
                sampled,
                preferred_element_type=jnp.float32,
            )
            summed = product_term if summed is None else summed + product_term
    return summed.reshape(tile_count, weight.shape[0], extent // 2, extent // 2)


def level_grads(hidden, cot_full, weight):
    tile_count, chan_count, extent = (hidden.shape[0], hidden.shape[1], hidden.shape[2])
    half = extent // 2
    cot_rows = cot_full.reshape(tile_count, cot_full.shape[1], -1)
    weight_rows = []
    spread_rows = []
    for row_tap in range(2):
        weight_cols = []
        spread_cols = []
        for col_tap in range(2):
            sampled = hidden[:, :, row_tap::2, col_tap::2].reshape(tile_count, chan_count, -1)
            weight_cols.append(
                jnp.einsum("nop,ncp->oc", cot_rows, sampled, preferred_element_type=jnp.float32)
            )
            spread = jnp.einsum(
                "oc,nop->ncp",
                weight[:, :, row_tap, col_tap],
                cot_rows,
                preferred_element_type=jnp.float32,
            )
            spread_cols.append(spread.reshape(tile_count, chan_count, half, half))
        weight_rows.append(jnp.stack(weight_cols, axis=-1))
        spread_rows.append(jnp.stack(spread_cols, axis=-1))
    grad_weight = jnp.stack(weight_rows, axis=2)
    grad_hidden = jnp.stack(spread_rows, axis=3).reshape(tile_count, chan_count, extent, extent)
    return (grad_weight, grad_hidden)


def conv_grads(padded, grad_full, weight):
    extent = padded.shape[2] - 2
    grad_padded = jnp.zeros(padded.shape, jnp.float32)
    weight_rows = []
    for row_tap in range(3):
        weight_cols = []
        for col_tap in range(3):
            window = padded[:, :, row_tap : row_tap + extent, col_tap : col_tap + extent]
            weight_cols.append(
                jnp.einsum("noxy,ncxy->oc", grad_full, window, preferred_element_type=jnp.float32)
            )
            spread = jnp.einsum(
                "oc,noxy->ncxy",
                weight[:, :, row_tap, col_tap],
                grad_full,
                preferred_element_type=jnp.float32,
            )
            grad_padded = grad_padded.at[
                :, :, row_tap : row_tap + extent, col_tap : col_tap + extent
            ].add(spread)
        weight_rows.append(jnp.stack(weight_cols, axis=-1))
    return (jnp.stack(weight_rows, axis=2), grad_padded)


def add_returned(grad_padded, returned):
    interior = grad_padded[:, :, 1:-1, 1:-1]
    interior = interior.at[:, :, 0, :].add(returned[:, 0])
    interior = interior.at[:, :, -1, :].add(returned[:, 1])
    interior = interior.at[:, :, :, 0].add(returned[:, 2])
    interior = interior.at[:, :, :, -1].add(returned[:, 3])
    return interior.astype(jnp.bfloat16)


def flatten_pixels(field):
    return field.reshape(field.shape[0], field.shape[1], -1)


def on_device_general(inputs, gluing, conv_weight, level_weight, cotangent):
    inputs = inputs.reshape(inputs.shape[0], inputs.shape[1], S, S)
    cotangent = cotangent.reshape(cotangent.shape[0], cotangent.shape[1], S // 2, S // 2)
    chan_width = inputs.shape[1]
    chan_first = lax.axis_index("chan") * chan_width
    tile_share = inputs.shape[0] // lax.axis_size("chan")
    tile_first = lax.axis_index("chan") * tile_share
    local_gluing = lax.dynamic_slice_in_dim(gluing, tile_first, tile_share, 0)
    picker = make_picker(local_gluing)
    whole_input, cot_full = (
        lax.all_to_all(inputs, "chan", split_axis=0, concat_axis=1, tiled=True),
        lax.all_to_all(cotangent, "chan", split_axis=0, concat_axis=1, tiled=True),
    )
    strips = edge_strips(whole_input)
    halo_cells = picker(
        jnp.zeros_like(strips),
        lax.all_gather(strips, ("tile", "chan"), axis=0, tiled=True),
        jnp.int32(0),
    )
    padded_whole = assemble(whole_input, orient(halo_cells, local_gluing))
    pre_act = conv_three(padded_whole, conv_weight)
    hidden = jax.nn.gelu(pre_act).astype(jnp.bfloat16)
    level_whole = conv_two(hidden, level_weight).astype(jnp.bfloat16)
    level = lax.all_to_all(level_whole, "chan", split_axis=1, concat_axis=0, tiled=True)
    grad_level, grad_hidden = level_grads(hidden, cot_full, level_weight)
    unused, pullback = jax.vjp(jax.nn.gelu, pre_act)
    grad_pre = pullback(grad_hidden)[0].astype(jnp.bfloat16)
    grad_conv, grad_padded = conv_grads(padded_whole, grad_pre, conv_weight)
    grad_conv, grad_level = lax.psum((grad_conv, grad_level), ("tile", "chan"))
    grad_conv = lax.dynamic_slice_in_dim(grad_conv, chan_first, chan_width, 1)
    grad_level = lax.dynamic_slice_in_dim(grad_level, chan_first, chan_width, 1)
    rims = border_strips(grad_padded).astype(jnp.bfloat16)
    returned = picker(
        jnp.zeros_like(rims),
        lax.all_gather(rims, ("tile", "chan"), axis=0, tiled=True),
        jnp.int32(0),
    )
    returned = orient(returned, local_gluing).astype(jnp.float32)
    grad_whole = add_returned(grad_padded, returned)
    grad_inputs = lax.all_to_all(grad_whole, "chan", split_axis=1, concat_axis=0, tiled=True)
    return (flatten_pixels(level), flatten_pixels(grad_inputs), grad_conv, grad_level)


MESH = pl.DeviceIdType.MESH
F32 = jnp.float32
BF16 = jnp.bfloat16
PIX = 1024
HALF = 32
ROOT = 0.7978845608028654
CUBIC = 0.044715


def split_matrix():
    lane = np.arange(512)
    row, col = lane // 64, lane % 64
    out = ((row % 2) * 2 + col % 2) * 128 + (row // 2) * 32 + col // 2
    matrix = np.zeros((512, 512), np.float32)
    matrix[lane, out] = 1.0
    return matrix


def spread_matrices():
    rows = np.zeros((128, PIX), np.float32)
    cols = np.zeros((128, PIX), np.float32)
    index = np.arange(HALF)
    rows[index, index] = 1.0
    rows[32 + index, 31 * HALF + index] = 1.0
    cols[64 + index, index * HALF] = 1.0
    cols[96 + index, index * HALF + 31] = 1.0
    return rows, cols


def strip_matrix():
    index = np.arange(64)
    slot = (index % 2) * 32 + index // 2
    matrix = np.zeros((4096, 256), np.float32)
    matrix[index, slot] = 1.0
    matrix[63 * 64 + index, 64 + slot] = 1.0
    matrix[index * 64, 128 + slot] = 1.0
    matrix[index * 64 + 63, 192 + slot] = 1.0
    return matrix


def dot(left, right):
    return jnp.dot(left, right, preferred_element_type=F32)


def dot_last(left, right):
    return lax.dot_general(left, right, (((1,), (1,)), ((), ())), preferred_element_type=F32)


def reverse_matrix():
    row = lax.broadcasted_iota(jnp.int32, (128, 128), 0)
    col = lax.broadcasted_iota(jnp.int32, (128, 128), 1)
    same = (row // 64) == (col // 64)
    return (same & ((row % 64) + (col % 64) == 63)).astype(F32).astype(BF16)


def route(codes, strips, source):
    strips = strips.astype(BF16)
    straight = (codes == 2 * source).astype(F32).astype(BF16)
    turned = (codes == 2 * source + 1).astype(F32).astype(BF16)
    reverse = dot(strips, reverse_matrix()).astype(BF16)
    return dot(straight, strips) + dot(turned, reverse)


def hail_all(me):
    barrier = pltpu.get_barrier_semaphore()

    def greet(step):
        other = lax.rem(me + step, 32)
        pl.semaphore_signal(
            barrier, inc=1, device_id=(other // 2, lax.rem(other, 2)), device_id_type=MESH
        )

    loop(1, 32, greet)


def await_all():
    pl.semaphore_wait(pltpu.get_barrier_semaphore(), 31)


def unpack(field, half, out_ref):
    line = lax.broadcasted_iota(jnp.int32, (256, 256), 0)
    lane = lax.broadcasted_iota(jnp.int32, (256, 256), 1)
    channel = line % 64
    source = ((channel % 32) // 2 * 2 + channel // 32) * 8 + half * 4 + line // 64
    flat = field.reshape(256, 128).astype(BF16)
    mine = dot((lane == source).astype(F32).astype(BF16), flat)
    odd = lax.broadcasted_iota(jnp.int32, (256, 64), 0) % 2 == 1
    mine = jnp.where(odd, mine[:, 64:], mine[:, :64])
    for b in range(2):
        out_ref[64 * b:64 * b + 64, :] = jnp.concatenate(
            [mine[64 * k:64 * k + 64, 32 * b:32 * b + 32] for k in range(4)], axis=1
        ).astype(BF16)


def pack(rims):
    sides = jnp.concatenate(
        [
            jnp.concatenate([rims[:64, 32 * k:32 * k + 32], rims[64:, 32 * k:32 * k + 32]], axis=1)
            for k in range(4)
        ],
        axis=0,
    ).astype(BF16)
    line = lax.broadcasted_iota(jnp.int32, (256, 256), 0)
    lane = lax.broadcasted_iota(jnp.int32, (256, 256), 1)
    device, side = line // 8, line % 8
    source = jnp.where(side < 4, side * 64 + (device % 2) * 32 + device // 2 * 2, -2)
    return jnp.concatenate(
        [dot((lane == source + k).astype(F32).astype(BF16), sides) for k in range(2)], axis=1
    )


def remote(src, dst, send, recv, tile, chan):
    return pltpu.make_async_remote_copy(
        src_ref=src, dst_ref=dst, send_sem=send, recv_sem=recv,
        device_id=(tile, chan), device_id_type=MESH,
    )


def loop(first, last, body):
    def step(index, carry):
        body(index)
        return carry

    lax.fori_loop(first, last, step, 0)


def gather_kernel(
    x_ref, cot_ref, strip_ref, codes_ref,
    xo_ref, co_ref, halo_ref, all_ref,
    strips_ref, held, routed, arrived,
    big_send, big_recv, one_send, one_recv, code_send, code_recv, two_send, two_recv,
):
    row, half = lax.axis_index("tile"), lax.axis_index("chan")
    me = row * 2 + half
    other = 1 - half
    hail_all(me)
    picked = dot(x_ref[...].reshape(64, 4096), strip_ref[...])
    sides = jnp.concatenate([picked[:, 64 * k:64 * k + 64] for k in range(4)], axis=0).astype(BF16)
    line = lax.broadcasted_iota(jnp.int32, (128, 256), 0)
    lane = lax.broadcasted_iota(jnp.int32, (128, 256), 1)
    first = (line % 4) * 64 + ((line // 4) % 2) * 32 + (line // 8) * 2
    strips_ref[...] = jnp.concatenate(
        [dot((lane == first + k).astype(F32).astype(BF16), sides) for k in range(2)], axis=1
    ).reshape(16, 8, 128)
    await_all()

    def to_row(step):
        j = lax.rem(row + step, 16)
        yield remote(codes_ref, all_ref.at[row], code_send.at[j], code_recv.at[row], j, half)
        yield remote(strips_ref.at[j], held.at[row], one_send.at[j], one_recv.at[row], j, half)

    def from_row(step):
        j = lax.rem(row + step, 16)
        yield remote(codes_ref, all_ref.at[j], code_send.at[j], code_recv.at[j], j, half)
        yield remote(strips_ref.at[j], held.at[j], one_send.at[j], one_recv.at[j], j, half)

    loop(1, 16, lambda step: [copy.start() for copy in to_row(step)])
    x_copy = remote(x_ref.at[other], xo_ref.at[half], big_send.at[0], big_recv.at[0], row, other)
    c_copy = remote(cot_ref.at[other], co_ref.at[half], big_send.at[1], big_recv.at[1], row, other)
    x_copy.start()
    held[row] = strips_ref[row]
    all_ref[row] = codes_ref[...]
    xo_ref[half] = x_ref[half]
    co_ref[half] = cot_ref[half]
    loop(1, 16, lambda step: [copy.wait_recv() for copy in from_row(step)])
    lane = lax.broadcasted_iota(jnp.int32, (128, 128), 1)
    answer = route(all_ref[...].reshape(128, 128), held[...].reshape(128, 128), lane)
    routed[...] = answer.reshape(16, 8, 128)

    def to_all(step):
        q = lax.rem(me + step, 32)
        return remote(
            routed.at[q // 2], arrived.at[me], two_send.at[q], two_recv.at[me], q // 2, lax.rem(q, 2)
        )

    def from_all(step):
        q = lax.rem(me + step, 32)
        return remote(
            routed.at[q // 2], arrived.at[q], two_send.at[q], two_recv.at[q], q // 2, lax.rem(q, 2)
        )

    loop(1, 32, lambda step: to_all(step).start())
    c_copy.start()
    arrived[me] = routed[row]
    loop(1, 32, lambda step: from_all(step).wait_recv())
    unpack(arrived[...], half, halo_ref)
    x_copy.wait()
    c_copy.wait()
    loop(1, 16, lambda step: [copy.wait_send() for copy in to_row(step)])
    loop(1, 32, lambda step: to_all(step).wait_send())


def masks():
    pixel = lax.broadcasted_iota(jnp.int32, (64, PIX), 1)
    return pixel < 32, pixel >= 992, (pixel % 32) == 0, (pixel % 32) == 31


def patches(planes, rows, cols, out_ref):
    top, low, left, right = masks()
    zero = jnp.zeros((64, PIX), F32)

    def ahead(value, by):
        return pltpu.roll(value, by % PIX, 1)

    def column(a, s):
        if s in (0, 1):
            return planes[a][s]
        beside = zero if cols is None else cols[a]
        if s < 0:
            return jnp.where(left, beside, ahead(planes[a][1], 1))
        return jnp.where(right, beside, ahead(planes[a][0], -1))

    def outer(s):
        if rows is None:
            return zero
        if s in (0, 1):
            return rows[s]
        if s < 0:
            return jnp.where(left, 0.0, ahead(rows[1], 1))
        return jnp.where(right, 0.0, ahead(rows[0], -1))

    for s in range(-1, 3):
        even, odd = column(0, s), column(1, s)
        edge = outer(s)
        parts = (
            jnp.where(top, edge, ahead(odd, 32)), even, odd, jnp.where(low, edge, ahead(even, -32))
        )
        for r in range(4):
            first = (r * 4 + s + 1) * 64
            out_ref[first:first + 64, :] = parts[r].astype(BF16)


def work_kernel(
    x_ref, cot_ref, halo_ref, taps_ref, turned_ref, lw_ref, lwt_ref, split_ref, rows_ref, cols_ref,
    level_ref, gi_ref, rims_ref, grads_ref,
    z_ref, zg_ref, wide_ref, back_ref, turn_ref,
):
    wide_ref[...] = jnp.zeros_like(wide_ref)
    back_ref[...] = jnp.zeros_like(back_ref)
    turn_ref[...] = jnp.zeros_like(turn_ref)
    for i in range(3):
        for j in range(3):
            tap, turned = taps_ref[i * 3 + j], turned_ref[i * 3 + j]
            for a in range(2):
                for b in range(2):
                    line, at = (a * 2 + b) * 64, ((a + i) * 4 + b + j) * 64
                    back_at = ((a + 2 - i) * 4 + b + 2 - j) * 64
                    wide_ref[line:line + 64, at:at + 64] = tap
                    turn_ref[at:at + 64, line:line + 64] = turned
                    back_ref[line:line + 64, back_at:back_at + 64] = turned
    x = x_ref[...]
    stacked = jnp.concatenate([x[:, 512 * k:512 * k + 512] for k in range(8)], axis=0)
    split = dot(stacked, split_ref[...])

    def plane(index):
        return jnp.concatenate(
            [split[64 * k:64 * k + 64, 128 * index:128 * index + 128] for k in range(8)], axis=1
        )

    halo = halo_ref[...]
    rows = dot(halo, rows_ref[...])
    cols = dot(halo, cols_ref[...])
    patches(
        [[plane(0), plane(1)], [plane(2), plane(3)]],
        [rows[:64], rows[64:]], [cols[:64], cols[64:]], z_ref,
    )
    pre = dot(wide_ref[...], z_ref[...])
    square = pre * pre
    bent = jnp.tanh(ROOT * pre * (1.0 + CUBIC * square))
    hidden = (0.5 * pre * (1.0 + bent)).astype(BF16)
    slope = 0.5 * (1.0 + bent) + 0.5 * pre * (1.0 - bent * bent) * ROOT * (1.0 + 3.0 * CUBIC * square)
    level_ref[...] = dot(lw_ref[...], hidden).astype(BF16)
    cot = cot_ref[...]
    level_grad = dot_last(hidden, cot)
    grads_ref[...] = jnp.zeros_like(grads_ref)

    def keep(h, first, rows, lanes, value):
        for core in range(2):
            low, high = max(first, 136 * core), min(first + rows, 136 * core + 136)
            if low < high:
                grads_ref[h * 2 + core, low - 136 * core:high - 136 * core, lanes] = (
                    value[low - first:high - first]
                )

    for k in range(4):
        for h in range(2):
            at = 64 * k + 32 * h
            keep(h, 144 + 32 * k, 32, slice(0, 128), level_grad[at:at + 32])
    grad_pre = (dot(lwt_ref[...], cot) * slope).astype(BF16)
    wide_grad = dot_last(z_ref[...], grad_pre)
    for i in range(3):
        for j in range(3):
            total = None
            for a in range(2):
                for b in range(2):
                    first, at = (a * 2 + b) * 64, ((a + i) * 4 + b + j) * 64
                    term = wide_grad[at:at + 64, first:first + 64]
                    total = term if total is None else total + term
            for h in range(2):
                for part in range(2):
                    at = 32 * h + 16 * part
                    keep(
                        h, 16 * (i * 3 + j), 16, slice(64 * part, 64 * part + 64), total[at:at + 16]
                    )
    wide = grad_pre.astype(F32)
    patches(
        [[wide[0:64], wide[64:128]], [wide[128:192], wide[192:256]]], None, None, zg_ref
    )
    gi_ref[...] = dot(back_ref[...], zg_ref[...])
    edge = dot_last(grad_pre, rows_ref[...] + cols_ref[...]).astype(BF16)
    spill = dot(turn_ref[...], edge)
    lane = lax.broadcasted_iota(jnp.int32, (64, 128), 1)

    def around(k):
        def block(r, s):
            first = (r * 4 + s) * 64
            return spill[first:first + 64, :]

        low = jnp.where(lane < 32, block(0, k), block(3, k))
        high = jnp.where(lane < 96, block(k, 0), block(k, 3))
        return jnp.where(lane < 64, low, high)

    inner = lane % 32
    before = jnp.where(inner == 0, 0.0, pltpu.roll(around(3), 1, 1))
    after = jnp.where(inner == 31, 0.0, pltpu.roll(around(0), 127, 1))
    rims_ref[...] = pack(jnp.concatenate([around(1) + before, around(2) + after], axis=0))


def return_kernel(
    level_ref, rims_ref, codes_ref, grads_ref, gi_ref, rows_ref, cols_ref, split_ref,
    lo_ref, out_ref, sums_ref,
    held, routed, arrived, back, mine, near, owned, far, total,
    big_send, big_recv, one_send, one_recv, two_send, two_recv,
    a_send, a_recv, b_send, b_recv, c_send, c_recv, d_send, d_recv,
):
    row, half = lax.axis_index("tile"), lax.axis_index("chan")
    me = row * 2 + half
    other = 1 - half
    core, chip = lax.rem(row, 2), row // 2
    mate = row + 1 - 2 * core
    hail_all(me)
    await_all()

    def place(step):
        q = lax.rem(me + step, 32)
        return q, q // 2, lax.rem(q, 2)

    def rim_to(step):
        q, j, c = place(step)
        return remote(rims_ref.at[q], held.at[me], one_send.at[q], one_recv.at[me], j, c)

    def rim_from(step):
        q, j, c = place(step)
        return remote(rims_ref.at[q], held.at[q], one_send.at[q], one_recv.at[q], j, c)

    loop(1, 32, lambda step: rim_to(step).start())
    whole = pl.ds(0, 136)
    near_copies = [
        remote(
            grads_ref.at[h * 2 + lax.rem(to, 2), whole], near.at[k, whole],
            a_send.at[k], a_recv.at[k], to, h,
        )
        for k, (to, h) in enumerate(((mate, half), (row, other), (mate, other)))
    ]
    for copy in near_copies:
        copy.start()
    held[me] = rims_ref[me]
    lo_ref[half] = level_ref[half]
    loop(1, 32, lambda step: rim_from(step).wait_recv())
    lane = lax.broadcasted_iota(jnp.int32, (128, 256), 1)
    codes = codes_ref[...].reshape(128, 128)
    codes = jnp.concatenate([codes, codes], axis=1)
    source = jnp.where((lane % 8) < 4, (lane // 8) * 4 + lane % 8, -1)
    answer = route(codes, held[...].reshape(256, 128), source)
    routed[...] = answer.reshape(16, 8, 128)

    def all_to(step):
        q, j, c = place(step)
        return remote(routed.at[j], arrived.at[me], two_send.at[q], two_recv.at[me], j, c)

    def all_from(step):
        q, j, c = place(step)
        return remote(routed.at[j], arrived.at[q], two_send.at[q], two_recv.at[q], j, c)

    loop(1, 32, lambda step: all_to(step).start())
    l_copy = remote(level_ref.at[other], lo_ref.at[half], big_send.at[0], big_recv.at[0], row, other)
    l_copy.start()
    arrived[me] = routed[row]

    for copy in near_copies:
        copy.wait_recv()
    quarter = grads_ref[half * 2 + core, 0:136, :]
    for k in range(3):
        quarter = quarter + near[k, 0:136, :]
    for k in range(5):
        owned[k] = quarter[24 * k:24 * k + 24]
    owned[5, 0:16, :] = quarter[120:136]
    owned[5, 16:24, :] = jnp.zeros((8, 128), F32)
    owned[6] = jnp.zeros((24, 128), F32)
    owned[7] = jnp.zeros((24, 128), F32)

    def part_to(step):
        j = lax.rem(chip + step, 8)
        return remote(owned.at[j], far.at[chip], b_send.at[j], b_recv.at[chip], j * 2 + core, half)

    def part_from(step):
        j = lax.rem(chip + step, 8)
        return remote(owned.at[j], far.at[j], b_send.at[j], b_recv.at[j], j * 2 + core, half)

    loop(1, 8, lambda step: part_to(step).start())
    far[chip] = owned[chip]

    loop(1, 32, lambda step: all_from(step).wait_recv())
    unpack(arrived[...], half, back)
    rows = dot(back[...], rows_ref[...])
    cols = dot(back[...], cols_ref[...])
    top, low, left, right = masks()
    planes = []
    for a in range(2):
        for b in range(2):
            first = (a * 2 + b) * 64
            field = gi_ref[first:first + 64, :]
            field = field + jnp.where(low if a else top, rows[b * 64:b * 64 + 64], 0.0)
            field = field + jnp.where(right if b else left, cols[a * 64:a * 64 + 64], 0.0)
            planes.append(field.astype(BF16))
    stacked = jnp.concatenate(
        [
            jnp.concatenate([part[:, 128 * k:128 * k + 128] for part in planes], axis=1)
            for k in range(8)
        ],
        axis=0,
    )
    joined = dot_last(stacked, split_ref[...]).astype(BF16)
    for k in range(8):
        for h in range(2):
            first = 64 * k + 32 * h
            mine[h, :, 512 * k:512 * k + 512] = joined[first:first + 32, :]
    g_copy = remote(mine.at[other], out_ref.at[half], big_send.at[1], big_recv.at[1], row, other)
    g_copy.start()
    out_ref[half] = mine[half]

    loop(1, 8, lambda step: part_from(step).wait_recv())
    total[...] = jnp.sum(far[...], axis=0)

    def sum_to(step):
        j = lax.rem(chip + step, 8)
        return remote(
            total, sums_ref.at[core, chip], c_send.at[j], c_recv.at[chip], j * 2 + core, half
        )

    def sum_from(step):
        j = lax.rem(chip + step, 8)
        return remote(total, sums_ref.at[core, j], c_send.at[j], c_recv.at[j], j * 2 + core, half)

    loop(1, 8, lambda step: sum_to(step).start())
    sums_ref[core, chip] = total[...]
    loop(1, 8, lambda step: sum_from(step).wait_recv())
    d_copy = remote(sums_ref.at[core], sums_ref.at[core], d_send, d_recv, mate, half)
    d_copy.start()
    loop(1, 32, lambda step: rim_to(step).wait_send())
    loop(1, 32, lambda step: all_to(step).wait_send())
    loop(1, 8, lambda step: part_to(step).wait_send())
    loop(1, 8, lambda step: sum_to(step).wait_send())
    for copy in near_copies:
        copy.wait_send()
    l_copy.wait()
    d_copy.wait()
    g_copy.wait()


def vmem(count):
    return [pl.BlockSpec(memory_space=pltpu.VMEM)] * count


def shape(dims, kind):
    return jax.ShapeDtypeStruct(dims, kind)


def params(mib, **extra):
    return pltpu.CompilerParams(vmem_limit_bytes=mib * 1024 * 1024, **extra)


def on_device_fast(inputs, gluing, conv_weight, level_weight, cotangent):
    dma = pltpu.SemaphoreType.DMA
    rows_np, cols_np = spread_matrices()
    rows_mat, cols_mat = jnp.asarray(rows_np, BF16), jnp.asarray(cols_np, BF16)
    split_mat = jnp.asarray(split_matrix(), BF16)
    taps = conv_weight.transpose(2, 3, 0, 1).reshape(9, 64, 64)
    turned = taps.transpose(0, 2, 1)
    lwt = level_weight.transpose(2, 3, 1, 0).reshape(256, 128)
    codes = ((gluing[:, :, 0] * 4 + gluing[:, :, 1]) * 2 + gluing[:, :, 2]).reshape(8, 1)
    codes = jnp.broadcast_to(codes, (8, 128))
    whole, cot, halo, all_codes = pl.pallas_call(
        gather_kernel,
        out_shape=(
            shape((2, 32, 4096), BF16), shape((2, 64, 1024), BF16),
            shape((128, 128), BF16), shape((16, 8, 128), jnp.int32),
        ),
        in_specs=vmem(4),
        out_specs=tuple(vmem(4)),
        scratch_shapes=[
            pltpu.VMEM((16, 8, 128), F32), pltpu.VMEM((16, 8, 128), F32),
            pltpu.VMEM((16, 8, 128), F32), pltpu.VMEM((32, 8, 128), F32),
            dma((2,)), dma((2,)), dma((16,)), dma((16,)), dma((16,)), dma((16,)), dma((32,)), dma((32,)),
        ],
        compiler_params=params(16, collective_id=0, has_side_effects=True),
        name="gather",
    )(inputs, cotangent, jnp.asarray(strip_matrix(), BF16), codes)
    level, gi, rims, grads = pl.pallas_call(
        work_kernel,
        out_shape=(
            shape((128, 1024), BF16), shape((256, 1024), F32), shape((256, 128), F32),
            shape((4, 192, 128), F32),
        ),
        in_specs=vmem(10),
        out_specs=tuple(vmem(4)),
        scratch_shapes=[
            pltpu.VMEM((1024, 1024), BF16), pltpu.VMEM((1024, 1024), BF16),
            pltpu.VMEM((256, 1024), BF16), pltpu.VMEM((256, 1024), BF16),
            pltpu.VMEM((1024, 256), BF16),
        ],
        compiler_params=params(26),
        name="work",
    )(
        whole.reshape(64, 4096), cot.reshape(128, 1024), halo, taps, turned, lwt.T, lwt,
        split_mat, rows_mat, cols_mat,
    )
    level, grad_inputs, sums = pl.pallas_call(
        return_kernel,
        out_shape=(
            shape((2, 64, 1024), BF16), shape((2, 32, 4096), BF16), shape((2, 8, 24, 128), F32),
        ),
        in_specs=vmem(8),
        out_specs=tuple(vmem(3)),
        scratch_shapes=[
            pltpu.VMEM((32, 8, 128), F32), pltpu.VMEM((16, 8, 128), F32),
            pltpu.VMEM((32, 8, 128), F32), pltpu.VMEM((128, 128), BF16),
            pltpu.VMEM((2, 32, 4096), BF16), pltpu.VMEM((3, 192, 128), F32),
            pltpu.VMEM((8, 24, 128), F32), pltpu.VMEM((8, 24, 128), F32), pltpu.VMEM((24, 128), F32),
            dma((2,)), dma((2,)), dma((32,)), dma((32,)), dma((32,)), dma((32,)),
            dma((3,)), dma((3,)), dma((8,)), dma((8,)), dma((8,)), dma((8,)), dma(()), dma(()),
        ],
        compiler_params=params(16, collective_id=1, has_side_effects=True),
        name="return",
    )(
        level.reshape(2, 64, 1024), rims.reshape(32, 8, 128), all_codes, grads, gi,
        rows_mat, cols_mat, split_mat,
    )
    sums = sums.reshape(2, 192, 128)[:, :136].reshape(272, 128)
    grad_conv = sums[:144].reshape(3, 3, 16, 2, 64).transpose(4, 3, 2, 0, 1).reshape(64, 32, 3, 3)
    grad_level = sums[144:].reshape(2, 2, 32, 128).transpose(3, 2, 0, 1)
    return level, grad_inputs, grad_conv, grad_level


def solution(mesh):
    fits = mesh.shape["tile"] == 16 and mesh.shape["chan"] == 2
    return jax.shard_map(
        on_device_fast if fits else on_device_general,
        mesh=mesh,
        in_specs=(
            P("tile", "chan", None),
            P("tile", None, None),
            P(),
            P(),
            P("tile", "chan", None),
        ),
        out_specs=(
            P("tile", "chan", None),
            P("tile", "chan", None),
            P(None, "chan", None, None),
            P(None, "chan", None, None),
        ),
        check_vma=False,
    )
```

```python
import functools

import jax
import jax.numpy as jnp
import numpy as np
from jax import lax
from jax.experimental import pallas as pl
from jax.experimental.pallas import tpu as pltpu
from jax.sharding import PartitionSpec as P

S = 64


def edge_strips(source):
    return jnp.stack(
        [source[:, :, 0, :], source[:, :, -1, :], source[:, :, :, 0], source[:, :, :, -1]], axis=1
    )


def border_strips(padded):
    return jnp.stack(
        [
            padded[:, :, 0, 1:-1],
            padded[:, :, -1, 1:-1],
            padded[:, :, 1:-1, 0],
            padded[:, :, 1:-1, -1],
        ],
        axis=1,
    )


def orient(strips, gluing):
    return jnp.where(gluing[:, :, 2][:, :, None, None] == 1, strips[..., ::-1], strips)


def make_picker(gluing):
    target = gluing[:, :, 0] * 4 + gluing[:, :, 1]

    def picker(current, received, first_row):
        strip_count = received.shape[0] * 4
        received_rows = received.reshape((strip_count,) + received.shape[2:])
        inside = (target >= 0) & (target < strip_count)
        chosen = jnp.take(received_rows, jnp.clip(target, 0, strip_count - 1), axis=0)
        return jnp.where(inside[:, :, None, None], chosen, current)

    return picker


def assemble(source, halo_cells):
    tile_count, chan_count = (source.shape[0], source.shape[1])
    corner = jnp.zeros((tile_count, chan_count, 1), source.dtype)
    top_row = jnp.concatenate([corner, halo_cells[:, 0], corner], axis=2)[:, :, None, :]
    low_row = jnp.concatenate([corner, halo_cells[:, 1], corner], axis=2)[:, :, None, :]
    middle = jnp.concatenate(
        [halo_cells[:, 2][:, :, :, None], source, halo_cells[:, 3][:, :, :, None]], axis=3
    )
    return jnp.concatenate([top_row, middle, low_row], axis=2)


def conv_three(padded, weight):
    extent = padded.shape[2] - 2
    summed = None
    for row_tap in range(3):
        for col_tap in range(3):
            product_term = jnp.einsum(
                "oc,ncxy->noxy",
                weight[:, :, row_tap, col_tap],
                padded[:, :, row_tap : row_tap + extent, col_tap : col_tap + extent],
                preferred_element_type=jnp.float32,
            )
            summed = product_term if summed is None else summed + product_term
    return summed


def conv_two(hidden, weight):
    tile_count, chan_count, extent = (hidden.shape[0], hidden.shape[1], hidden.shape[2])
    summed = None
    for row_tap in range(2):
        for col_tap in range(2):
            sampled = hidden[:, :, row_tap::2, col_tap::2].reshape(tile_count, chan_count, -1)
            product_term = jnp.einsum(
                "oc,ncp->nop",
                weight[:, :, row_tap, col_tap],
                sampled,
                preferred_element_type=jnp.float32,
            )
            summed = product_term if summed is None else summed + product_term
    return summed.reshape(tile_count, weight.shape[0], extent // 2, extent // 2)


def level_grads(hidden, cot_full, weight):
    tile_count, chan_count, extent = (hidden.shape[0], hidden.shape[1], hidden.shape[2])
    half = extent // 2
    cot_rows = cot_full.reshape(tile_count, cot_full.shape[1], -1)
    weight_rows = []
    spread_rows = []
    for row_tap in range(2):
        weight_cols = []
        spread_cols = []
        for col_tap in range(2):
            sampled = hidden[:, :, row_tap::2, col_tap::2].reshape(tile_count, chan_count, -1)
            weight_cols.append(
                jnp.einsum("nop,ncp->oc", cot_rows, sampled, preferred_element_type=jnp.float32)
            )
            spread = jnp.einsum(
                "oc,nop->ncp",
                weight[:, :, row_tap, col_tap],
                cot_rows,
                preferred_element_type=jnp.float32,
            )
            spread_cols.append(spread.reshape(tile_count, chan_count, half, half))
        weight_rows.append(jnp.stack(weight_cols, axis=-1))
        spread_rows.append(jnp.stack(spread_cols, axis=-1))
    grad_weight = jnp.stack(weight_rows, axis=2)
    grad_hidden = jnp.stack(spread_rows, axis=3).reshape(tile_count, chan_count, extent, extent)
    return (grad_weight, grad_hidden)


def conv_grads(padded, grad_full, weight):
    extent = padded.shape[2] - 2
    grad_padded = jnp.zeros(padded.shape, jnp.float32)
    weight_rows = []
    for row_tap in range(3):
        weight_cols = []
        for col_tap in range(3):
            window = padded[:, :, row_tap : row_tap + extent, col_tap : col_tap + extent]
            weight_cols.append(
                jnp.einsum("noxy,ncxy->oc", grad_full, window, preferred_element_type=jnp.float32)
            )
            spread = jnp.einsum(
                "oc,noxy->ncxy",
                weight[:, :, row_tap, col_tap],
                grad_full,
                preferred_element_type=jnp.float32,
            )
            grad_padded = grad_padded.at[
                :, :, row_tap : row_tap + extent, col_tap : col_tap + extent
            ].add(spread)
        weight_rows.append(jnp.stack(weight_cols, axis=-1))
    return (jnp.stack(weight_rows, axis=2), grad_padded)


def add_returned(grad_padded, returned):
    interior = grad_padded[:, :, 1:-1, 1:-1]
    interior = interior.at[:, :, 0, :].add(returned[:, 0])
    interior = interior.at[:, :, -1, :].add(returned[:, 1])
    interior = interior.at[:, :, :, 0].add(returned[:, 2])
    interior = interior.at[:, :, :, -1].add(returned[:, 3])
    return interior.astype(jnp.bfloat16)


def flatten_pixels(field):
    return field.reshape(field.shape[0], field.shape[1], -1)


def on_device_general(inputs, gluing, conv_weight, level_weight, cotangent):
    inputs = inputs.reshape(inputs.shape[0], inputs.shape[1], S, S)
    cotangent = cotangent.reshape(cotangent.shape[0], cotangent.shape[1], S // 2, S // 2)
    chan_width = inputs.shape[1]
    chan_first = lax.axis_index("chan") * chan_width
    tile_share = inputs.shape[0] // lax.axis_size("chan")
    tile_first = lax.axis_index("chan") * tile_share
    local_gluing = lax.dynamic_slice_in_dim(gluing, tile_first, tile_share, 0)
    picker = make_picker(local_gluing)
    whole_input, cot_full = (
        lax.all_to_all(inputs, "chan", split_axis=0, concat_axis=1, tiled=True),
        lax.all_to_all(cotangent, "chan", split_axis=0, concat_axis=1, tiled=True),
    )
    strips = edge_strips(whole_input)
    halo_cells = picker(
        jnp.zeros_like(strips),
        lax.all_gather(strips, ("tile", "chan"), axis=0, tiled=True),
        jnp.int32(0),
    )
    padded_whole = assemble(whole_input, orient(halo_cells, local_gluing))
    pre_act = conv_three(padded_whole, conv_weight)
    hidden = jax.nn.gelu(pre_act).astype(jnp.bfloat16)
    level_whole = conv_two(hidden, level_weight).astype(jnp.bfloat16)
    level = lax.all_to_all(level_whole, "chan", split_axis=1, concat_axis=0, tiled=True)
    grad_level, grad_hidden = level_grads(hidden, cot_full, level_weight)
    unused, pullback = jax.vjp(jax.nn.gelu, pre_act)
    grad_pre = pullback(grad_hidden)[0].astype(jnp.bfloat16)
    grad_conv, grad_padded = conv_grads(padded_whole, grad_pre, conv_weight)
    grad_conv, grad_level = lax.psum((grad_conv, grad_level), ("tile", "chan"))
    grad_conv = lax.dynamic_slice_in_dim(grad_conv, chan_first, chan_width, 1)
    grad_level = lax.dynamic_slice_in_dim(grad_level, chan_first, chan_width, 1)
    rims = border_strips(grad_padded).astype(jnp.bfloat16)
    returned = picker(
        jnp.zeros_like(rims),
        lax.all_gather(rims, ("tile", "chan"), axis=0, tiled=True),
        jnp.int32(0),
    )
    returned = orient(returned, local_gluing).astype(jnp.float32)
    grad_whole = add_returned(grad_padded, returned)
    grad_inputs = lax.all_to_all(grad_whole, "chan", split_axis=1, concat_axis=0, tiled=True)
    return (flatten_pixels(level), flatten_pixels(grad_inputs), grad_conv, grad_level)


MESH = pl.DeviceIdType.MESH
F32 = jnp.float32
BF16 = jnp.bfloat16
PIX = 1024
HALF = 32
ROOT = 0.7978845608028654
CUBIC = 0.044715


def split_matrix():
    lane = np.arange(512)
    row, col = lane // 64, lane % 64
    out = ((row % 2) * 2 + col % 2) * 128 + (row // 2) * 32 + col // 2
    matrix = np.zeros((512, 512), np.float32)
    matrix[lane, out] = 1.0
    return matrix


def spread_matrices():
    rows = np.zeros((128, PIX), np.float32)
    cols = np.zeros((128, PIX), np.float32)
    index = np.arange(HALF)
    rows[index, index] = 1.0
    rows[32 + index, 31 * HALF + index] = 1.0
    cols[64 + index, index * HALF] = 1.0
    cols[96 + index, index * HALF + 31] = 1.0
    return rows, cols


def dot(left, right):
    return jnp.dot(left, right, preferred_element_type=F32)


def dot_last(left, right):
    return lax.dot_general(left, right, (((1,), (1,)), ((), ())), preferred_element_type=F32)


def reverse_matrix():
    row = lax.broadcasted_iota(jnp.int32, (128, 128), 0)
    col = lax.broadcasted_iota(jnp.int32, (128, 128), 1)
    same = (row // 64) == (col // 64)
    return (same & ((row % 64) + (col % 64) == 63)).astype(F32).astype(BF16)


def route(codes, strips, source):
    strips = strips.astype(BF16)
    straight = (codes == 2 * source).astype(F32).astype(BF16)
    turned = (codes == 2 * source + 1).astype(F32).astype(BF16)
    reverse = dot(strips, reverse_matrix()).astype(BF16)
    return dot(straight, strips) + dot(turned, reverse)


def hail_all(me):
    barrier = pltpu.get_barrier_semaphore()

    def greet(step):
        other = lax.rem(me + step, 32)
        pl.semaphore_signal(
            barrier, inc=1, device_id=(other // 2, lax.rem(other, 2)), device_id_type=MESH
        )

    loop(1, 32, greet)


def await_all():
    pl.semaphore_wait(pltpu.get_barrier_semaphore(), 31)


def pick(line_count, lane_count, source):
    lane = lax.broadcasted_iota(jnp.int32, (line_count, lane_count), 1)
    line = lax.broadcasted_iota(jnp.int32, (line_count, lane_count), 0)
    return (lane == source(line)).astype(F32).astype(BF16)


def unpack(field, out_ref):
    def source(line):
        channel = line % 64
        return ((channel % 32) // 2 * 2 + channel // 32) * 4 + line // 64

    mine = dot(pick(256, 128, source), field.astype(BF16))
    odd = lax.broadcasted_iota(jnp.int32, (256, 64), 0) % 2 == 1
    mine = jnp.where(odd, mine[:, 64:], mine[:, :64])
    for b in range(2):
        out_ref[64 * b:64 * b + 64, :] = jnp.concatenate(
            [mine[64 * k:64 * k + 64, 32 * b:32 * b + 32] for k in range(4)], axis=1
        ).astype(BF16)


def pack(rims):
    sides = jnp.concatenate(
        [
            jnp.concatenate([rims[:64, 32 * k:32 * k + 32], rims[64:, 32 * k:32 * k + 32]], axis=1)
            for k in range(4)
        ],
        axis=0,
    ).astype(BF16)

    def source(line):
        device = line // 4
        return line % 4 * 64 + (device % 2) * 32 + device // 2 * 2

    return jnp.concatenate(
        [dot(pick(128, 256, lambda line: source(line) + k), sides) for k in range(2)], axis=1
    )


def to_slabs(ref, value):
    for k in range(32):
        ref[k] = value[4 * k:4 * k + 4]


def remote(src, dst, send, recv, tile, chan):
    return pltpu.make_async_remote_copy(
        src_ref=src, dst_ref=dst, send_sem=send, recv_sem=recv,
        device_id=(tile, chan), device_id_type=MESH,
    )


def loop(first, last, body):
    def step(index, carry):
        body(index)
        return carry

    lax.fori_loop(first, last, step, 0)


def masks():
    pixel = lax.broadcasted_iota(jnp.int32, (64, PIX), 1)
    return pixel < 32, pixel >= 992, (pixel % 32) == 0, (pixel % 32) == 31


def patches(planes, rows, cols, out_ref):
    top, low, left, right = masks()
    zero = jnp.zeros((64, PIX), F32)

    def ahead(value, by):
        return pltpu.roll(value, by % PIX, 1)

    def column(a, s):
        if s in (0, 1):
            return planes[a][s]
        beside = zero if cols is None else cols[a]
        if s < 0:
            return jnp.where(left, beside, ahead(planes[a][1], 1))
        return jnp.where(right, beside, ahead(planes[a][0], -1))

    def outer(s):
        if rows is None:
            return zero
        if s in (0, 1):
            return rows[s]
        if s < 0:
            return jnp.where(left, 0.0, ahead(rows[1], 1))
        return jnp.where(right, 0.0, ahead(rows[0], -1))

    for s in range(-1, 3):
        even, odd = column(0, s), column(1, s)
        edge = outer(s)
        parts = (
            jnp.where(top, edge, ahead(odd, 32)), even, odd, jnp.where(low, edge, ahead(even, -32))
        )
        for r in range(4):
            first = (r * 4 + s + 1) * 64
            out_ref[first:first + 64, :] = parts[r].astype(BF16)


def whole_kernel(
    x_any, cot_any, codes_ref, taps_any, lw_any, lwt_any, split_any, rows_any, cols_any,
    lo_ref, out_ref, sums_ref,
    x_ref, px_ref, xo_ref, co_ref, taps_ref, lw_ref, lwt_ref, split_ref, rows_ref, cols_ref,
    strips_ref, held, all_ref, routed, arrived, halo_ref,
    z_ref, zg_ref, wide_ref, back_ref, turn_ref, level_ref, gi_ref, grads_ref,
    rims_ref, rim_held, rim_routed, rim_arrived, back, mine, near, owned, far, total,
    in_sem, big_send, big_recv, code_send, code_recv, one_send, one_recv, two_send, two_recv,
    three_send, three_recv, four_send, four_recv,
    a_send, a_recv, b_send, b_recv, c_send, c_recv, d_send, d_recv,
):
    row, half = lax.axis_index("tile"), lax.axis_index("chan")
    me = row * 2 + half
    other = 1 - half
    core, chip = lax.rem(row, 2), row // 2
    mate = row + 1 - 2 * core
    hail_all(me)
    loads = [
        pltpu.make_async_copy(src, dst, in_sem.at[k])
        for k, (src, dst) in enumerate(
            (
                (x_any, x_ref), (split_any, split_ref), (rows_any, rows_ref), (cols_any, cols_ref),
                (taps_any, taps_ref), (lw_any, lw_ref), (lwt_any, lwt_ref),
                (cot_any.at[half], co_ref.at[half]),
            )
        )
    ]
    for load in loads:
        load.start()

    def place(step):
        q = lax.rem(me + step, 32)
        return q, q // 2, lax.rem(q, 2)

    def in_row(step):
        return lax.rem(row + step, 16)

    for load in loads[:4]:
        load.wait()
    x = x_ref[...].reshape(64, 4096)
    stacked = jnp.concatenate([x[:, 512 * k:512 * k + 512] for k in range(8)], axis=0)
    split = dot(stacked, split_ref[...]).astype(BF16)
    planes = [
        jnp.concatenate(
            [split[64 * k:64 * k + 64, 128 * index:128 * index + 128] for k in range(8)], axis=1
        )
        for index in range(4)
    ]
    for index in range(4):
        for t in range(2):
            px_ref[t, index] = planes[index][32 * t:32 * t + 32]
    edges = [dot_last(part, rows_ref[...] + cols_ref[...]) for part in planes]
    sides = jnp.concatenate(
        [
            jnp.concatenate([edges[index][:, 32 * s:32 * s + 32] for index in pair], axis=1)
            for s, pair in enumerate(((0, 1), (2, 3), (0, 2), (1, 3)))
        ],
        axis=0,
    ).astype(BF16)

    def strip_source(line):
        return (line % 4) * 64 + ((line // 4) % 2) * 32 + (line // 8) * 2

    strips_ref[...] = jnp.concatenate(
        [dot(pick(128, 256, lambda line: strip_source(line) + k), sides) for k in range(2)], axis=1
    ).reshape(16, 8, 128)
    await_all()

    def code_copy(step, slot):
        j = in_row(step)
        return remote(
            codes_ref, all_ref.at[slot(j)], code_send.at[j], code_recv.at[slot(j)], j, half
        )

    def strip_copy(step, slot):
        j = in_row(step)
        return remote(
            strips_ref.at[j], held.at[slot(j)], one_send.at[j], one_recv.at[slot(j)], j, half
        )

    def mine_in_row(j):
        return row

    def theirs(j):
        return j

    def start_strips(step):
        strip_copy(step, mine_in_row).start()
        code_copy(step, mine_in_row).start()

    def await_strips(step):
        strip_copy(step, theirs).wait_recv()
        code_copy(step, theirs).wait_recv()

    loop(1, 16, start_strips)
    x_copy = remote(px_ref.at[other], xo_ref.at[half], big_send.at[0], big_recv.at[0], row, other)
    x_copy.start()
    held[row] = strips_ref[row]
    all_ref[row] = codes_ref[...]
    xo_ref[half] = px_ref[half]
    for load in loads[4:]:
        load.wait()
    wide_ref[...] = jnp.zeros_like(wide_ref)
    back_ref[...] = jnp.zeros_like(back_ref)
    turn_ref[...] = jnp.zeros_like(turn_ref)
    one = pick(64, 64, lambda line: line)
    for i in range(3):
        for j in range(3):
            tap = taps_ref[i * 3 + j]
            turned = dot_last(one, tap).astype(BF16)
            for a in range(2):
                for b in range(2):
                    line, at = (a * 2 + b) * 64, ((a + i) * 4 + b + j) * 64
                    back_at = ((a + 2 - i) * 4 + b + 2 - j) * 64
                    wide_ref[line:line + 64, at:at + 64] = tap
                    turn_ref[at:at + 64, line:line + 64] = turned
                    back_ref[line:line + 64, back_at:back_at + 64] = turned
    loop(1, 16, await_strips)
    lane = lax.broadcasted_iota(jnp.int32, (128, 128), 1)
    codes = all_ref[...].reshape(128, 128)
    to_slabs(routed, route(codes, held[...].reshape(128, 128), lane))

    def halo_copy(step, slot):
        q, j, c = place(step)
        return remote(routed.at[q], arrived.at[slot(q)], two_send.at[q], two_recv.at[slot(q)], j, c)

    def myself(q):
        return me

    loop(1, 32, lambda step: halo_copy(step, myself).start())
    c_copy = remote(cot_any.at[other], co_ref.at[half], big_send.at[1], big_recv.at[1], row, other)
    c_copy.start()
    arrived[me] = routed[me]
    loop(1, 32, lambda step: halo_copy(step, theirs).wait_recv())
    unpack(arrived[...].reshape(128, 128), halo_ref)
    halo = halo_ref[...]
    rows = dot(halo, rows_ref[...])
    cols = dot(halo, cols_ref[...])
    x_copy.wait_recv()
    parts = [
        jnp.concatenate([xo_ref[0, index], xo_ref[1, index]], axis=0).astype(F32) for index in range(4)
    ]
    patches([parts[:2], parts[2:]], [rows[:64], rows[64:]], [cols[:64], cols[64:]], z_ref)
    pre = dot(wide_ref[...], z_ref[...])
    square = pre * pre
    bent = jnp.tanh(ROOT * pre * (1.0 + CUBIC * square))
    hidden = (0.5 * pre * (1.0 + bent)).astype(BF16)
    slope = 0.5 * (1.0 + bent) + 0.5 * pre * (1.0 - bent * bent) * ROOT * (1.0 + 3.0 * CUBIC * square)
    level_ref[...] = dot(lw_ref[...], hidden).astype(BF16).reshape(2, 64, 1024)
    c_copy.wait_recv()
    l_copy = remote(level_ref.at[other], lo_ref.at[half], big_send.at[2], big_recv.at[2], row, other)
    cot = co_ref[...].reshape(128, 1024)
    grad_pre = (dot(lwt_ref[...], cot) * slope).astype(BF16)

    edge = dot_last(grad_pre, rows_ref[...] + cols_ref[...]).astype(BF16)
    spill = dot(turn_ref[...], edge)
    small = lax.broadcasted_iota(jnp.int32, (64, 128), 1)

    def around(k):
        def block(r, s):
            first = (r * 4 + s) * 64
            return spill[first:first + 64, :]

        low = jnp.where(small < 32, block(0, k), block(3, k))
        high = jnp.where(small < 96, block(k, 0), block(k, 3))
        return jnp.where(small < 64, low, high)

    inner = small % 32
    before = jnp.where(inner == 0, 0.0, pltpu.roll(around(3), 1, 1))
    after = jnp.where(inner == 31, 0.0, pltpu.roll(around(0), 127, 1))
    to_slabs(rims_ref, pack(jnp.concatenate([around(1) + before, around(2) + after], axis=0)))

    def rim_copy(step, slot):
        q, j, c = place(step)
        return remote(
            rims_ref.at[q], rim_held.at[slot(q)], three_send.at[q], three_recv.at[slot(q)], j, c
        )

    loop(1, 32, lambda step: rim_copy(step, myself).start())
    l_copy.start()
    rim_held[me] = rims_ref[me]
    lo_ref[half] = level_ref[half]

    def keep(h, first, count, lanes, value):
        for k in range(2):
            low, high = max(first, 136 * k), min(first + count, 136 * k + 136)
            if low < high:
                grads_ref[h * 2 + k, low - 136 * k:high - 136 * k, lanes] = (
                    value[low - first:high - first]
                )

    level_grad = dot_last(hidden, cot)
    for k in range(4):
        for h in range(2):
            at = 64 * k + 32 * h
            keep(h, 144 + 32 * k, 32, slice(0, 128), level_grad[at:at + 32])
    wide_grad = dot_last(z_ref[...], grad_pre)
    for i in range(3):
        for j in range(3):
            sum_tap = None
            for a in range(2):
                for b in range(2):
                    first, at = (a * 2 + b) * 64, ((a + i) * 4 + b + j) * 64
                    term = wide_grad[at:at + 64, first:first + 64]
                    sum_tap = term if sum_tap is None else sum_tap + term
            for h in range(2):
                for part in range(2):
                    at = 32 * h + 16 * part
                    keep(
                        h, 16 * (i * 3 + j), 16, slice(64 * part, 64 * part + 64), sum_tap[at:at + 16]
                    )
    near_copies = [
        remote(
            grads_ref.at[h * 2 + lax.rem(to, 2)], near.at[k], a_send.at[k], a_recv.at[k], to, h
        )
        for k, (to, h) in enumerate(((mate, half), (row, other), (mate, other)))
    ]
    for copy in near_copies:
        copy.start()

    loop(1, 32, lambda step: rim_copy(step, theirs).wait_recv())
    to_slabs(rim_routed, route(codes, rim_held[...].reshape(128, 128), lane))

    def back_copy(step, slot):
        q, j, c = place(step)
        return remote(
            rim_routed.at[q], rim_arrived.at[slot(q)], four_send.at[q], four_recv.at[slot(q)], j, c
        )

    loop(1, 32, lambda step: back_copy(step, myself).start())
    rim_arrived[me] = rim_routed[me]
    field = grad_pre.astype(F32)
    patches([[field[0:64], field[64:128]], [field[128:192], field[192:256]]], None, None, zg_ref)
    gi_ref[...] = dot(back_ref[...], zg_ref[...])

    for copy in near_copies:
        copy.wait_recv()
    quarter = grads_ref[half * 2 + core]
    for k in range(3):
        quarter = quarter + near[k]
    for k in range(5):
        owned[k] = quarter[24 * k:24 * k + 24]
    owned[5, 0:16, :] = quarter[120:136]
    owned[5, 16:24, :] = jnp.zeros((8, 128), F32)
    owned[6] = jnp.zeros((24, 128), F32)
    owned[7] = jnp.zeros((24, 128), F32)

    def part_copy(step, slot):
        j = lax.rem(chip + step, 8)
        return remote(
            owned.at[j], far.at[slot(j)], b_send.at[j], b_recv.at[slot(j)], j * 2 + core, half
        )

    def my_chip(j):
        return chip

    loop(1, 8, lambda step: part_copy(step, my_chip).start())
    far[chip] = owned[chip]

    loop(1, 32, lambda step: back_copy(step, theirs).wait_recv())
    unpack(rim_arrived[...].reshape(128, 128), back)
    rows = dot(back[...], rows_ref[...])
    cols = dot(back[...], cols_ref[...])
    top, low, left, right = masks()
    planes = []
    for a in range(2):
        for b in range(2):
            first = (a * 2 + b) * 64
            field = gi_ref[first:first + 64, :]
            field = field + jnp.where(low if a else top, rows[b * 64:b * 64 + 64], 0.0)
            field = field + jnp.where(right if b else left, cols[a * 64:a * 64 + 64], 0.0)
            planes.append(field.astype(BF16))
    stacked = jnp.concatenate(
        [
            jnp.concatenate([part[:, 128 * k:128 * k + 128] for part in planes], axis=1)
            for k in range(8)
        ],
        axis=0,
    )
    joined = dot_last(stacked, split_ref[...]).astype(BF16)
    for k in range(8):
        for h in range(2):
            first = 64 * k + 32 * h
            mine[h, :, 512 * k:512 * k + 512] = joined[first:first + 32, :]
    g_copy = remote(mine.at[other], out_ref.at[half], big_send.at[3], big_recv.at[3], row, other)
    g_copy.start()
    out_ref[half] = mine[half]

    loop(1, 8, lambda step: part_copy(step, theirs).wait_recv())
    total[...] = jnp.sum(far[...], axis=0)

    def sum_copy(step, slot):
        j = lax.rem(chip + step, 8)
        return remote(
            total, sums_ref.at[core, slot(j)], c_send.at[j], c_recv.at[slot(j)], j * 2 + core, half
        )

    loop(1, 8, lambda step: sum_copy(step, my_chip).start())
    sums_ref[core, chip] = total[...]
    loop(1, 8, lambda step: sum_copy(step, theirs).wait_recv())
    d_copy = remote(sums_ref.at[core], sums_ref.at[core], d_send, d_recv, mate, half)
    d_copy.start()

    def sent_in_row(step):
        strip_copy(step, mine_in_row).wait_send()
        code_copy(step, mine_in_row).wait_send()

    def sent_to_all(step):
        halo_copy(step, myself).wait_send()
        rim_copy(step, myself).wait_send()
        back_copy(step, myself).wait_send()

    def sent_to_chips(step):
        part_copy(step, my_chip).wait_send()
        sum_copy(step, my_chip).wait_send()

    loop(1, 16, sent_in_row)
    loop(1, 32, sent_to_all)
    loop(1, 8, sent_to_chips)
    for copy in near_copies:
        copy.wait_send()
    x_copy.wait_send()
    c_copy.wait_send()
    l_copy.wait()
    d_copy.wait()
    g_copy.wait()


def vmem(count):
    return [pl.BlockSpec(memory_space=pltpu.VMEM)] * count


def shape(dims, kind):
    return jax.ShapeDtypeStruct(dims, kind)


def params(mib, **extra):
    return pltpu.CompilerParams(vmem_limit_bytes=mib * 1024 * 1024, **extra)


def on_device_fast(inputs, gluing, conv_weight, level_weight, cotangent):
    dma = pltpu.SemaphoreType.DMA
    rows_np, cols_np = spread_matrices()
    taps = conv_weight.transpose(2, 3, 0, 1).reshape(9, 64, 64)
    lwt = level_weight.transpose(2, 3, 1, 0).reshape(256, 128)
    codes = ((gluing[:, :, 0] * 4 + gluing[:, :, 1]) * 2 + gluing[:, :, 2]).reshape(8, 1)
    codes = jnp.broadcast_to(codes, (8, 128))
    hbm = pl.BlockSpec(memory_space=pltpu.HBM)
    eights, fours = (16, 8, 128), (32, 4, 128)
    level, grad_inputs, sums = pl.pallas_call(
        whole_kernel,
        out_shape=(
            shape((2, 64, 1024), BF16), shape((2, 32, 4096), BF16), shape((2, 8, 24, 128), F32),
        ),
        in_specs=[hbm, hbm] + vmem(1) + [hbm] * 6,
        out_specs=tuple(vmem(3)),
        scratch_shapes=[
            pltpu.VMEM(dims, kind)
            for dims, kind in (
                ((2, 32, 4096), BF16), ((2, 4, 32, 1024), BF16), ((2, 4, 32, 1024), BF16),
                ((2, 64, 1024), BF16), ((9, 64, 64), BF16), ((128, 256), BF16), ((256, 128), BF16),
                ((512, 512), BF16), ((128, 1024), BF16), ((128, 1024), BF16),
                (eights, F32), (eights, F32), (eights, jnp.int32), (fours, F32), (fours, F32),
                ((128, 128), BF16),
                ((1024, 1024), BF16), ((1024, 1024), BF16), ((256, 1024), BF16), ((256, 1024), BF16),
                ((1024, 256), BF16), ((2, 64, 1024), BF16), ((256, 1024), F32), ((4, 136, 128), F32),
                (fours, F32), (fours, F32), (fours, F32), (fours, F32), ((128, 128), BF16),
                ((2, 32, 4096), BF16), ((3, 136, 128), F32),
                ((8, 24, 128), F32), ((8, 24, 128), F32), ((24, 128), F32),
            )
        ]
        + [
            dma((count,))
            for count in (8, 4, 4, 16, 16, 16, 16, 32, 32, 32, 32, 32, 32, 3, 3, 8, 8, 8, 8)
        ]
        + [dma(()), dma(())],
        compiler_params=params(44, collective_id=0, has_side_effects=True),
        name="whole",
    )(
        inputs, cotangent, codes, taps, lwt.T, lwt, jnp.asarray(split_matrix(), BF16),
        jnp.asarray(rows_np, BF16), jnp.asarray(cols_np, BF16),
    )
    sums = sums.reshape(2, 192, 128)[:, :136].reshape(272, 128)
    grad_conv = sums[:144].reshape(3, 3, 16, 2, 64).transpose(4, 3, 2, 0, 1).reshape(64, 32, 3, 3)
    grad_level = sums[144:].reshape(2, 2, 32, 128).transpose(3, 2, 0, 1)
    return level, grad_inputs, grad_conv, grad_level


def solution(mesh):
    fits = mesh.shape["tile"] == 16 and mesh.shape["chan"] == 2
    return jax.shard_map(
        on_device_fast if fits else on_device_general,
        mesh=mesh,
        in_specs=(
            P("tile", "chan", None),
            P("tile", None, None),
            P(),
            P(),
            P("tile", "chan", None),
        ),
        out_specs=(
            P("tile", "chan", None),
            P("tile", "chan", None),
            P(None, "chan", None, None),
            P(None, "chan", None, None),
        ),
        check_vma=False,
    )
```

```python
import jax
import jax.numpy as jnp
from jax import lax
from jax.experimental import pallas as pl
from jax.experimental.pallas import tpu as pltpu
from jax.sharding import PartitionSpec as P

S = 64


def edge_strips(source):
    return jnp.stack(
        [source[:, :, 0, :], source[:, :, -1, :], source[:, :, :, 0], source[:, :, :, -1]], axis=1
    )


def border_strips(padded):
    return jnp.stack(
        [
            padded[:, :, 0, 1:-1],
            padded[:, :, -1, 1:-1],
            padded[:, :, 1:-1, 0],
            padded[:, :, 1:-1, -1],
        ],
        axis=1,
    )


def orient(strips, gluing):
    return jnp.where(gluing[:, :, 2][:, :, None, None] == 1, strips[..., ::-1], strips)


def make_picker(gluing):
    target = gluing[:, :, 0] * 4 + gluing[:, :, 1]

    def picker(current, received, first_row):
        strip_count = received.shape[0] * 4
        received_rows = received.reshape((strip_count,) + received.shape[2:])
        inside = (target >= 0) & (target < strip_count)
        chosen = jnp.take(received_rows, jnp.clip(target, 0, strip_count - 1), axis=0)
        return jnp.where(inside[:, :, None, None], chosen, current)

    return picker


def assemble(source, halo_cells):
    tile_count, chan_count = (source.shape[0], source.shape[1])
    corner = jnp.zeros((tile_count, chan_count, 1), source.dtype)
    top_row = jnp.concatenate([corner, halo_cells[:, 0], corner], axis=2)[:, :, None, :]
    low_row = jnp.concatenate([corner, halo_cells[:, 1], corner], axis=2)[:, :, None, :]
    middle = jnp.concatenate(
        [halo_cells[:, 2][:, :, :, None], source, halo_cells[:, 3][:, :, :, None]], axis=3
    )
    return jnp.concatenate([top_row, middle, low_row], axis=2)


def conv_three(padded, weight):
    extent = padded.shape[2] - 2
    summed = None
    for row_tap in range(3):
        for col_tap in range(3):
            product_term = jnp.einsum(
                "oc,ncxy->noxy",
                weight[:, :, row_tap, col_tap],
                padded[:, :, row_tap : row_tap + extent, col_tap : col_tap + extent],
                preferred_element_type=jnp.float32,
            )
            summed = product_term if summed is None else summed + product_term
    return summed


def conv_two(hidden, weight):
    tile_count, chan_count, extent = (hidden.shape[0], hidden.shape[1], hidden.shape[2])
    summed = None
    for row_tap in range(2):
        for col_tap in range(2):
            sampled = hidden[:, :, row_tap::2, col_tap::2].reshape(tile_count, chan_count, -1)
            product_term = jnp.einsum(
                "oc,ncp->nop",
                weight[:, :, row_tap, col_tap],
                sampled,
                preferred_element_type=jnp.float32,
            )
            summed = product_term if summed is None else summed + product_term
    return summed.reshape(tile_count, weight.shape[0], extent // 2, extent // 2)


def level_grads(hidden, cot_full, weight):
    tile_count, chan_count, extent = (hidden.shape[0], hidden.shape[1], hidden.shape[2])
    half = extent // 2
    cot_rows = cot_full.reshape(tile_count, cot_full.shape[1], -1)
    weight_rows = []
    spread_rows = []
    for row_tap in range(2):
        weight_cols = []
        spread_cols = []
        for col_tap in range(2):
            sampled = hidden[:, :, row_tap::2, col_tap::2].reshape(tile_count, chan_count, -1)
            weight_cols.append(
                jnp.einsum("nop,ncp->oc", cot_rows, sampled, preferred_element_type=jnp.float32)
            )
            spread = jnp.einsum(
                "oc,nop->ncp",
                weight[:, :, row_tap, col_tap],
                cot_rows,
                preferred_element_type=jnp.float32,
            )
            spread_cols.append(spread.reshape(tile_count, chan_count, half, half))
        weight_rows.append(jnp.stack(weight_cols, axis=-1))
        spread_rows.append(jnp.stack(spread_cols, axis=-1))
    grad_weight = jnp.stack(weight_rows, axis=2)
    grad_hidden = jnp.stack(spread_rows, axis=3).reshape(tile_count, chan_count, extent, extent)
    return (grad_weight, grad_hidden)


def conv_grads(padded, grad_full, weight):
    extent = padded.shape[2] - 2
    grad_padded = jnp.zeros(padded.shape, jnp.float32)
    weight_rows = []
    for row_tap in range(3):
        weight_cols = []
        for col_tap in range(3):
            window = padded[:, :, row_tap : row_tap + extent, col_tap : col_tap + extent]
            weight_cols.append(
                jnp.einsum("noxy,ncxy->oc", grad_full, window, preferred_element_type=jnp.float32)
            )
            spread = jnp.einsum(
                "oc,noxy->ncxy",
                weight[:, :, row_tap, col_tap],
                grad_full,
                preferred_element_type=jnp.float32,
            )
            grad_padded = grad_padded.at[
                :, :, row_tap : row_tap + extent, col_tap : col_tap + extent
            ].add(spread)
        weight_rows.append(jnp.stack(weight_cols, axis=-1))
    return (jnp.stack(weight_rows, axis=2), grad_padded)


def add_returned(grad_padded, returned):
    interior = grad_padded[:, :, 1:-1, 1:-1]
    interior = interior.at[:, :, 0, :].add(returned[:, 0])
    interior = interior.at[:, :, -1, :].add(returned[:, 1])
    interior = interior.at[:, :, :, 0].add(returned[:, 2])
    interior = interior.at[:, :, :, -1].add(returned[:, 3])
    return interior.astype(jnp.bfloat16)


def flatten_pixels(field):
    return field.reshape(field.shape[0], field.shape[1], -1)


def on_device_general(inputs, gluing, conv_weight, level_weight, cotangent):
    inputs = inputs.reshape(inputs.shape[0], inputs.shape[1], S, S)
    cotangent = cotangent.reshape(cotangent.shape[0], cotangent.shape[1], S // 2, S // 2)
    chan_width = inputs.shape[1]
    chan_first = lax.axis_index("chan") * chan_width
    tile_share = inputs.shape[0] // lax.axis_size("chan")
    tile_first = lax.axis_index("chan") * tile_share
    local_gluing = lax.dynamic_slice_in_dim(gluing, tile_first, tile_share, 0)
    picker = make_picker(local_gluing)
    whole_input, cot_full = (
        lax.all_to_all(inputs, "chan", split_axis=0, concat_axis=1, tiled=True),
        lax.all_to_all(cotangent, "chan", split_axis=0, concat_axis=1, tiled=True),
    )
    strips = edge_strips(whole_input)
    halo_cells = picker(
        jnp.zeros_like(strips),
        lax.all_gather(strips, ("tile", "chan"), axis=0, tiled=True),
        jnp.int32(0),
    )
    padded_whole = assemble(whole_input, orient(halo_cells, local_gluing))
    pre_act = conv_three(padded_whole, conv_weight)
    hidden = jax.nn.gelu(pre_act).astype(jnp.bfloat16)
    level_whole = conv_two(hidden, level_weight).astype(jnp.bfloat16)
    level = lax.all_to_all(level_whole, "chan", split_axis=1, concat_axis=0, tiled=True)
    grad_level, grad_hidden = level_grads(hidden, cot_full, level_weight)
    unused, pullback = jax.vjp(jax.nn.gelu, pre_act)
    grad_pre = pullback(grad_hidden)[0].astype(jnp.bfloat16)
    grad_conv, grad_padded = conv_grads(padded_whole, grad_pre, conv_weight)
    grad_conv, grad_level = lax.psum((grad_conv, grad_level), ("tile", "chan"))
    grad_conv = lax.dynamic_slice_in_dim(grad_conv, chan_first, chan_width, 1)
    grad_level = lax.dynamic_slice_in_dim(grad_level, chan_first, chan_width, 1)
    rims = border_strips(grad_padded).astype(jnp.bfloat16)
    returned = picker(
        jnp.zeros_like(rims),
        lax.all_gather(rims, ("tile", "chan"), axis=0, tiled=True),
        jnp.int32(0),
    )
    returned = orient(returned, local_gluing).astype(jnp.float32)
    grad_whole = add_returned(grad_padded, returned)
    grad_inputs = lax.all_to_all(grad_whole, "chan", split_axis=1, concat_axis=0, tiled=True)
    return (flatten_pixels(level), flatten_pixels(grad_inputs), grad_conv, grad_level)


MESH = pl.DeviceIdType.MESH
F32 = jnp.float32
BF16 = jnp.bfloat16
PIX = 1024
HALF = 32
ROOT = 0.7978845608028654
CUBIC = 0.044715


def dot(left, right):
    return jnp.dot(left, right, preferred_element_type=F32)


def dot_last(left, right):
    return lax.dot_general(left, right, (((1,), (1,)), ((), ())), preferred_element_type=F32)


def reverse_matrix():
    row = lax.broadcasted_iota(jnp.int32, (128, 128), 0)
    col = lax.broadcasted_iota(jnp.int32, (128, 128), 1)
    same = (row // 64) == (col // 64)
    return (same & ((row % 64) + (col % 64) == 63)).astype(F32).astype(BF16)


def route(codes, strips, source):
    strips = strips.astype(BF16)
    straight = (codes == 2 * source).astype(F32).astype(BF16)
    turned = (codes == 2 * source + 1).astype(F32).astype(BF16)
    reverse = dot(strips, reverse_matrix()).astype(BF16)
    return dot(straight, strips) + dot(turned, reverse)


def to_others(row, half, body):
    def step(index):
        j = lax.rem(row + index, 16)
        body(j * 2 + half, j, half)
        body(j * 2 + 1 - half, j, 1 - half)

    loop(1, 16, step)
    body(row * 2 + 1 - half, row, 1 - half)


def hail_all(row, half):
    barrier = pltpu.get_barrier_semaphore()
    to_others(
        row, half,
        lambda q, j, c: pl.semaphore_signal(barrier, inc=1, device_id=(j, c), device_id_type=MESH),
    )


def await_all():
    pl.semaphore_wait(pltpu.get_barrier_semaphore(), 31)


def pick(line_count, lane_count, source):
    lane = lax.broadcasted_iota(jnp.int32, (line_count, lane_count), 1)
    line = lax.broadcasted_iota(jnp.int32, (line_count, 1), 0)
    return (lane == source(line)).astype(F32).astype(BF16)


def split_source(line):
    row, col = line // 64, line % 64
    return ((row % 2) * 2 + col % 2) * 128 + (row // 2) * 32 + col // 2


def rows_source(line):
    return jnp.where(line < 32, line, jnp.where(line < 64, line + 960, -1))


def cols_source(line):
    return jnp.where(line < 64, -1, jnp.where(line < 96, (line - 64) * 32, (line - 96) * 32 + 31))


def unpack(field, out_ref):
    def source(line):
        channel = line % 64
        return ((channel % 32) // 2 * 2 + channel // 32) * 4 + line // 64

    mine = dot(pick(256, 128, source), field.astype(BF16))
    odd = lax.broadcasted_iota(jnp.int32, (256, 64), 0) % 2 == 1
    mine = jnp.where(odd, mine[:, 64:], mine[:, :64])
    for b in range(2):
        out_ref[64 * b:64 * b + 64, :] = jnp.concatenate(
            [mine[64 * k:64 * k + 64, 32 * b:32 * b + 32] for k in range(4)], axis=1
        ).astype(BF16)


def pack(rims):
    sides = jnp.concatenate(
        [
            jnp.concatenate([rims[:64, 32 * k:32 * k + 32], rims[64:, 32 * k:32 * k + 32]], axis=1)
            for k in range(4)
        ],
        axis=0,
    ).astype(BF16)

    def source(line):
        device = line // 4
        return line % 4 * 64 + (device % 2) * 32 + device // 2 * 2

    return jnp.concatenate(
        [dot(pick(128, 256, lambda line: source(line) + k), sides) for k in range(2)], axis=1
    )


def to_slabs(ref, value):
    for k in range(32):
        ref[k] = value[4 * k:4 * k + 4]


def remote(src, dst, send, recv, tile, chan):
    return pltpu.make_async_remote_copy(
        src_ref=src, dst_ref=dst, send_sem=send, recv_sem=recv,
        device_id=(tile, chan), device_id_type=MESH,
    )


def loop(first, last, body):
    def step(index, carry):
        body(index)
        return carry

    lax.fori_loop(first, last, step, 0)


def masks():
    pixel = lax.broadcasted_iota(jnp.int32, (64, PIX), 1)
    return pixel < 32, pixel >= 992, (pixel % 32) == 0, (pixel % 32) == 31


def patches(planes, rows, cols, out_ref):
    top, low, left, right = masks()
    zero = jnp.zeros((64, PIX), F32)

    def ahead(value, by):
        return pltpu.roll(value, by % PIX, 1)

    def column(a, s):
        if s in (0, 1):
            return planes[a][s]
        beside = zero if cols is None else cols[a]
        if s < 0:
            return jnp.where(left, beside, ahead(planes[a][1], 1))
        return jnp.where(right, beside, ahead(planes[a][0], -1))

    def outer(s):
        if rows is None:
            return zero
        if s in (0, 1):
            return rows[s]
        if s < 0:
            return jnp.where(left, 0.0, ahead(rows[1], 1))
        return jnp.where(right, 0.0, ahead(rows[0], -1))

    for s in range(-1, 3):
        even, odd = column(0, s), column(1, s)
        edge = outer(s)
        parts = (
            jnp.where(top, edge, ahead(odd, 32)), even, odd, jnp.where(low, edge, ahead(even, -32))
        )
        for r in range(4):
            first = (r * 4 + s + 1) * 64
            out_ref[first:first + 64, :] = parts[r].astype(BF16)


def whole_kernel(
    x_any, cot_any, codes_ref, taps_any, lw_any, lwt_any,
    lo_ref, out_ref, sums_ref,
    x_ref, px_ref, xo_ref, co_ref, taps_ref, lw_ref, lwt_ref, split_ref, rows_ref, cols_ref,
    strips_ref, held, all_ref, routed, arrived, halo_ref,
    z_ref, zg_ref, wide_ref, back_ref, turn_ref, level_ref, gi_ref, grads_ref,
    rims_ref, rim_held, rim_routed, rim_arrived, back, mine, near, owned, far, total,
    in_sem, big_send, big_recv, code_send, code_recv, one_send, one_recv, two_send, two_recv,
    three_send, three_recv, four_send, four_recv,
    a_send, a_recv, b_send, b_recv, c_send, c_recv, d_send, d_recv,
):
    row, half = lax.axis_index("tile"), lax.axis_index("chan")
    me = row * 2 + half
    other = 1 - half
    core, chip = lax.rem(row, 2), row // 2
    mate = row + 1 - 2 * core
    hail_all(row, half)
    loads = [
        pltpu.make_async_copy(src, dst, in_sem.at[k])
        for k, (src, dst) in enumerate(
            (
                (x_any, x_ref),
                (taps_any, taps_ref), (lw_any, lw_ref), (lwt_any, lwt_ref),
                (cot_any.at[half], co_ref.at[half]),
            )
        )
    ]
    for load in loads:
        load.start()

    split_ref[...] = pick(512, 512, split_source)
    rows_ref[...] = pick(128, PIX, rows_source)
    cols_ref[...] = pick(128, PIX, cols_source)

    def send_all(src, dst, send, recv):
        to_others(row, half, lambda q, j, c: remote(src.at[q], dst.at[me], send, recv, j, c).start())
        dst[me] = src[me]
        return remote(src.at[pl.ds(0, 31)], dst.at[pl.ds(0, 31)], send, recv, row, other)

    def send_chips(pick_src, dst, send, recv):
        def step(index):
            j = lax.rem(chip + index, 8)
            remote(pick_src(j), dst.at[chip], send, recv, j * 2 + core, half).start()

        loop(1, 8, step)
        return remote(dst.at[pl.ds(0, 7)], dst.at[pl.ds(0, 7)], send, recv, mate, half)

    for load in loads[:1]:
        load.wait()
    x = x_ref[...].reshape(64, 4096)
    stacked = jnp.concatenate([x[:, 512 * k:512 * k + 512] for k in range(8)], axis=0)
    split = dot(stacked, split_ref[...]).astype(BF16)
    planes = [
        jnp.concatenate(
            [split[64 * k:64 * k + 64, 128 * index:128 * index + 128] for k in range(8)], axis=1
        )
        for index in range(4)
    ]
    for index in range(4):
        for t in range(2):
            px_ref[t, index] = planes[index][32 * t:32 * t + 32]
    edges = [dot_last(part, rows_ref[...] + cols_ref[...]) for part in planes]
    sides = jnp.concatenate(
        [
            jnp.concatenate([edges[index][:, 32 * s:32 * s + 32] for index in pair], axis=1)
            for s, pair in enumerate(((0, 1), (2, 3), (0, 2), (1, 3)))
        ],
        axis=0,
    ).astype(BF16)

    def strip_source(line):
        return (line % 4) * 64 + ((line // 4) % 2) * 32 + (line // 8) * 2

    strips_ref[...] = jnp.concatenate(
        [dot(pick(128, 256, lambda line: strip_source(line) + k), sides) for k in range(2)], axis=1
    ).reshape(16, 8, 128)
    await_all()

    def start_strips(index):
        j = lax.rem(row + index, 16)
        remote(codes_ref, all_ref.at[row], code_send, code_recv, j, half).start()
        remote(strips_ref.at[j], held.at[row], one_send, one_recv, j, half).start()

    loop(1, 16, start_strips)
    most = pl.ds(0, 15)
    code_all = remote(all_ref.at[most], all_ref.at[most], code_send, code_recv, row, other)
    strip_all = remote(strips_ref.at[most], held.at[most], one_send, one_recv, row, other)
    x_copy = remote(px_ref.at[other], xo_ref.at[half], big_send.at[0], big_recv.at[0], row, other)
    x_copy.start()
    held[row] = strips_ref[row]
    all_ref[row] = codes_ref[...]
    xo_ref[half] = px_ref[half]
    for load in loads[1:]:
        load.wait()
    wide_ref[...] = jnp.zeros_like(wide_ref)
    back_ref[...] = jnp.zeros_like(back_ref)
    turn_ref[...] = jnp.zeros_like(turn_ref)
    one = pick(64, 64, lambda line: line)
    for i in range(3):
        for j in range(3):
            tap = taps_ref[i * 3 + j]
            turned = dot_last(one, tap).astype(BF16)
            for a in range(2):
                for b in range(2):
                    line, at = (a * 2 + b) * 64, ((a + i) * 4 + b + j) * 64
                    back_at = ((a + 2 - i) * 4 + b + 2 - j) * 64
                    wide_ref[line:line + 64, at:at + 64] = tap
                    turn_ref[at:at + 64, line:line + 64] = turned
                    back_ref[line:line + 64, back_at:back_at + 64] = turned
    strip_all.wait_recv()
    code_all.wait_recv()
    lane = lax.broadcasted_iota(jnp.int32, (128, 128), 1)
    codes = all_ref[...].reshape(128, 128)
    to_slabs(routed, route(codes, held[...].reshape(128, 128), lane))

    halo_all = send_all(routed, arrived, two_send, two_recv)
    c_copy = remote(cot_any.at[other], co_ref.at[half], big_send.at[1], big_recv.at[1], row, other)
    c_copy.start()
    halo_all.wait_recv()
    unpack(arrived[...].reshape(128, 128), halo_ref)
    halo = halo_ref[...]
    rows = dot(halo, rows_ref[...])
    cols = dot(halo, cols_ref[...])
    x_copy.wait_recv()
    parts = [
        jnp.concatenate([xo_ref[0, index], xo_ref[1, index]], axis=0).astype(F32) for index in range(4)
    ]
    patches([parts[:2], parts[2:]], [rows[:64], rows[64:]], [cols[:64], cols[64:]], z_ref)
    pre = dot(wide_ref[...], z_ref[...])
    square = pre * pre
    bent = jnp.tanh(ROOT * pre * (1.0 + CUBIC * square))
    hidden = (0.5 * pre * (1.0 + bent)).astype(BF16)
    slope = 0.5 * (1.0 + bent) + 0.5 * pre * (1.0 - bent * bent) * ROOT * (1.0 + 3.0 * CUBIC * square)
    level_ref[...] = dot(lw_ref[...], hidden).astype(BF16).reshape(2, 64, 1024)
    c_copy.wait_recv()
    l_copy = remote(level_ref.at[other], lo_ref.at[half], big_send.at[2], big_recv.at[2], row, other)
    cot = co_ref[...].reshape(128, 1024)
    grad_pre = (dot(lwt_ref[...], cot) * slope).astype(BF16)

    edge = dot_last(grad_pre, rows_ref[...] + cols_ref[...]).astype(BF16)
    spill = dot(turn_ref[...], edge)
    small = lax.broadcasted_iota(jnp.int32, (64, 128), 1)

    def around(k):
        def block(r, s):
            first = (r * 4 + s) * 64
            return spill[first:first + 64, :]

        low = jnp.where(small < 32, block(0, k), block(3, k))
        high = jnp.where(small < 96, block(k, 0), block(k, 3))
        return jnp.where(small < 64, low, high)

    inner = small % 32
    before = jnp.where(inner == 0, 0.0, pltpu.roll(around(3), 1, 1))
    after = jnp.where(inner == 31, 0.0, pltpu.roll(around(0), 127, 1))
    to_slabs(rims_ref, pack(jnp.concatenate([around(1) + before, around(2) + after], axis=0)))

    rim_all = send_all(rims_ref, rim_held, three_send, three_recv)
    l_copy.start()
    lo_ref[half] = level_ref[half]

    def keep(h, first, count, lanes, value):
        for k in range(2):
            low, high = max(first, 136 * k), min(first + count, 136 * k + 136)
            if low < high:
                grads_ref[h * 2 + k, low - 136 * k:high - 136 * k, lanes] = (
                    value[low - first:high - first]
                )

    level_grad = dot_last(hidden, cot)
    for k in range(4):
        for h in range(2):
            at = 64 * k + 32 * h
            keep(h, 144 + 32 * k, 32, slice(0, 128), level_grad[at:at + 32])
    wide_grad = dot_last(z_ref[...], grad_pre)
    for i in range(3):
        for j in range(3):
            sum_tap = None
            for a in range(2):
                for b in range(2):
                    first, at = (a * 2 + b) * 64, ((a + i) * 4 + b + j) * 64
                    term = wide_grad[at:at + 64, first:first + 64]
                    sum_tap = term if sum_tap is None else sum_tap + term
            for h in range(2):
                for part in range(2):
                    at = 32 * h + 16 * part
                    keep(
                        h, 16 * (i * 3 + j), 16, slice(64 * part, 64 * part + 64), sum_tap[at:at + 16]
                    )
    near_copies = [
        remote(
            grads_ref.at[h * 2 + lax.rem(to, 2)], near.at[k], a_send.at[k], a_recv.at[k], to, h
        )
        for k, (to, h) in enumerate(((mate, half), (row, other), (mate, other)))
    ]
    for copy in near_copies:
        copy.start()

    rim_all.wait_recv()
    to_slabs(rim_routed, route(codes, rim_held[...].reshape(128, 128), lane))

    back_all = send_all(rim_routed, rim_arrived, four_send, four_recv)
    field = grad_pre.astype(F32)
    patches([[field[0:64], field[64:128]], [field[128:192], field[192:256]]], None, None, zg_ref)
    gi_ref[...] = dot(back_ref[...], zg_ref[...])

    for copy in near_copies:
        copy.wait_recv()
    quarter = grads_ref[half * 2 + core]
    for k in range(3):
        quarter = quarter + near[k]
    for k in range(5):
        owned[k] = quarter[24 * k:24 * k + 24]
    owned[5, 0:16, :] = quarter[120:136]
    owned[5, 16:24, :] = jnp.zeros((8, 128), F32)
    owned[6] = jnp.zeros((24, 128), F32)
    owned[7] = jnp.zeros((24, 128), F32)

    part_all = send_chips(lambda j: owned.at[j], far, b_send, b_recv)
    far[chip] = owned[chip]

    back_all.wait_recv()
    unpack(rim_arrived[...].reshape(128, 128), back)
    rows = dot(back[...], rows_ref[...])
    cols = dot(back[...], cols_ref[...])
    top, low, left, right = masks()
    planes = []
    for a in range(2):
        for b in range(2):
            first = (a * 2 + b) * 64
            field = gi_ref[first:first + 64, :]
            field = field + jnp.where(low if a else top, rows[b * 64:b * 64 + 64], 0.0)
            field = field + jnp.where(right if b else left, cols[a * 64:a * 64 + 64], 0.0)
            planes.append(field.astype(BF16))
    stacked = jnp.concatenate(
        [
            jnp.concatenate([part[:, 128 * k:128 * k + 128] for part in planes], axis=1)
            for k in range(8)
        ],
        axis=0,
    )
    joined = dot_last(stacked, split_ref[...]).astype(BF16)
    for k in range(8):
        for h in range(2):
            first = 64 * k + 32 * h
            mine[h, :, 512 * k:512 * k + 512] = joined[first:first + 32, :]
    g_copy = remote(mine.at[other], out_ref.at[half], big_send.at[3], big_recv.at[3], row, other)
    g_copy.start()
    out_ref[half] = mine[half]

    part_all.wait_recv()
    total[...] = jnp.sum(far[...], axis=0)

    sum_all = send_chips(lambda j: total, sums_ref.at[core], c_send, c_recv)
    sums_ref[core, chip] = total[...]
    sum_all.wait_recv()
    d_copy = remote(sums_ref.at[core], sums_ref.at[core], d_send, d_recv, mate, half)
    d_copy.start()

    for copies in (code_all, strip_all, halo_all, rim_all, back_all, part_all, sum_all):
        copies.wait_send()
    for copy in near_copies:
        copy.wait_send()
    x_copy.wait_send()
    c_copy.wait_send()
    l_copy.wait()
    d_copy.wait()
    g_copy.wait()


def vmem(count):
    return [pl.BlockSpec(memory_space=pltpu.VMEM)] * count


def shape(dims, kind):
    return jax.ShapeDtypeStruct(dims, kind)


def params(mib, **extra):
    return pltpu.CompilerParams(vmem_limit_bytes=mib * 1024 * 1024, **extra)


def on_device_fast(inputs, gluing, conv_weight, level_weight, cotangent):
    dma = pltpu.SemaphoreType.DMA
    taps = conv_weight.transpose(2, 3, 0, 1).reshape(9, 64, 64)
    lwt = level_weight.transpose(2, 3, 1, 0).reshape(256, 128)
    codes = ((gluing[:, :, 0] * 4 + gluing[:, :, 1]) * 2 + gluing[:, :, 2]).reshape(8, 1)
    codes = jnp.broadcast_to(codes, (8, 128))
    hbm = pl.BlockSpec(memory_space=pltpu.HBM)
    eights, fours = (16, 8, 128), (32, 4, 128)
    level, grad_inputs, sums = pl.pallas_call(
        whole_kernel,
        out_shape=(
            shape((2, 64, 1024), BF16), shape((2, 32, 4096), BF16), shape((2, 8, 24, 128), F32),
        ),
        in_specs=[hbm, hbm] + vmem(1) + [hbm] * 3,
        out_specs=tuple(vmem(3)),
        scratch_shapes=[
            pltpu.VMEM(dims, kind)
            for dims, kind in (
                ((2, 32, 4096), BF16), ((2, 4, 32, 1024), BF16), ((2, 4, 32, 1024), BF16),
                ((2, 64, 1024), BF16), ((9, 64, 64), BF16), ((128, 256), BF16), ((256, 128), BF16),
                ((512, 512), BF16), ((128, 1024), BF16), ((128, 1024), BF16),
                (eights, F32), (eights, F32), (eights, jnp.int32), (fours, F32), (fours, F32),
                ((128, 128), BF16),
                ((1024, 1024), BF16), ((1024, 1024), BF16), ((256, 1024), BF16), ((256, 1024), BF16),
                ((1024, 256), BF16), ((2, 64, 1024), BF16), ((256, 1024), F32), ((4, 136, 128), F32),
                (fours, F32), (fours, F32), (fours, F32), (fours, F32), ((128, 128), BF16),
                ((2, 32, 4096), BF16), ((3, 136, 128), F32),
                ((8, 24, 128), F32), ((8, 24, 128), F32), ((24, 128), F32),
            )
        ]
        + [
            dma((count,)) if count else dma(())
            for count in (5, 4, 4, 0, 0, 0, 0, 0, 0, 0, 0, 0, 0, 3, 3, 0, 0, 0, 0, 0, 0)
        ],
        compiler_params=params(53, collective_id=0, has_side_effects=True),
        name="whole",
    )(
        inputs, cotangent, codes, taps, lwt.T, lwt,
    )
    sums = sums.reshape(2, 192, 128)[:, :136].reshape(272, 128)
    grad_conv = sums[:144].reshape(3, 3, 16, 2, 64).transpose(4, 3, 2, 0, 1).reshape(64, 32, 3, 3)
    grad_level = sums[144:].reshape(2, 2, 32, 128).transpose(3, 2, 0, 1)
    return level, grad_inputs, grad_conv, grad_level


def solution(mesh):
    fits = mesh.shape["tile"] == 16 and mesh.shape["chan"] == 2
    return jax.shard_map(
        on_device_fast if fits else on_device_general,
        mesh=mesh,
        in_specs=(
            P("tile", "chan", None),
            P("tile", None, None),
            P(),
            P(),
            P("tile", "chan", None),
        ),
        out_specs=(
            P("tile", "chan", None),
            P("tile", "chan", None),
            P(None, "chan", None, None),
            P(None, "chan", None, None),
        ),
        check_vma=False,
    )
```

```python
import jax
import jax.numpy as jnp
from jax import lax
from jax.experimental import pallas as pl
from jax.experimental.pallas import tpu as pltpu
from jax.sharding import PartitionSpec as P

S = 64


def edge_strips(source):
    return jnp.stack(
        [source[:, :, 0, :], source[:, :, -1, :], source[:, :, :, 0], source[:, :, :, -1]], axis=1
    )


def border_strips(padded):
    return jnp.stack(
        [
            padded[:, :, 0, 1:-1],
            padded[:, :, -1, 1:-1],
            padded[:, :, 1:-1, 0],
            padded[:, :, 1:-1, -1],
        ],
        axis=1,
    )


def orient(strips, gluing):
    return jnp.where(gluing[:, :, 2][:, :, None, None] == 1, strips[..., ::-1], strips)


def make_picker(gluing):
    target = gluing[:, :, 0] * 4 + gluing[:, :, 1]

    def picker(current, received, first_row):
        strip_count = received.shape[0] * 4
        received_rows = received.reshape((strip_count,) + received.shape[2:])
        inside = (target >= 0) & (target < strip_count)
        chosen = jnp.take(received_rows, jnp.clip(target, 0, strip_count - 1), axis=0)
        return jnp.where(inside[:, :, None, None], chosen, current)

    return picker


def assemble(source, halo_cells):
    tile_count, chan_count = (source.shape[0], source.shape[1])
    corner = jnp.zeros((tile_count, chan_count, 1), source.dtype)
    top_row = jnp.concatenate([corner, halo_cells[:, 0], corner], axis=2)[:, :, None, :]
    low_row = jnp.concatenate([corner, halo_cells[:, 1], corner], axis=2)[:, :, None, :]
    middle = jnp.concatenate(
        [halo_cells[:, 2][:, :, :, None], source, halo_cells[:, 3][:, :, :, None]], axis=3
    )
    return jnp.concatenate([top_row, middle, low_row], axis=2)


def conv_three(padded, weight):
    extent = padded.shape[2] - 2
    summed = None
    for row_tap in range(3):
        for col_tap in range(3):
            product_term = jnp.einsum(
                "oc,ncxy->noxy",
                weight[:, :, row_tap, col_tap],
                padded[:, :, row_tap : row_tap + extent, col_tap : col_tap + extent],
                preferred_element_type=jnp.float32,
            )
            summed = product_term if summed is None else summed + product_term
    return summed


def conv_two(hidden, weight):
    tile_count, chan_count, extent = (hidden.shape[0], hidden.shape[1], hidden.shape[2])
    summed = None
    for row_tap in range(2):
        for col_tap in range(2):
            sampled = hidden[:, :, row_tap::2, col_tap::2].reshape(tile_count, chan_count, -1)
            product_term = jnp.einsum(
                "oc,ncp->nop",
                weight[:, :, row_tap, col_tap],
                sampled,
                preferred_element_type=jnp.float32,
            )
            summed = product_term if summed is None else summed + product_term
    return summed.reshape(tile_count, weight.shape[0], extent // 2, extent // 2)


def level_grads(hidden, cot_full, weight):
    tile_count, chan_count, extent = (hidden.shape[0], hidden.shape[1], hidden.shape[2])
    half = extent // 2
    cot_rows = cot_full.reshape(tile_count, cot_full.shape[1], -1)
    weight_rows = []
    spread_rows = []
    for row_tap in range(2):
        weight_cols = []
        spread_cols = []
        for col_tap in range(2):
            sampled = hidden[:, :, row_tap::2, col_tap::2].reshape(tile_count, chan_count, -1)
            weight_cols.append(
                jnp.einsum("nop,ncp->oc", cot_rows, sampled, preferred_element_type=jnp.float32)
            )
            spread = jnp.einsum(
                "oc,nop->ncp",
                weight[:, :, row_tap, col_tap],
                cot_rows,
                preferred_element_type=jnp.float32,
            )
            spread_cols.append(spread.reshape(tile_count, chan_count, half, half))
        weight_rows.append(jnp.stack(weight_cols, axis=-1))
        spread_rows.append(jnp.stack(spread_cols, axis=-1))
    grad_weight = jnp.stack(weight_rows, axis=2)
    grad_hidden = jnp.stack(spread_rows, axis=3).reshape(tile_count, chan_count, extent, extent)
    return (grad_weight, grad_hidden)


def conv_grads(padded, grad_full, weight):
    extent = padded.shape[2] - 2
    grad_padded = jnp.zeros(padded.shape, jnp.float32)
    weight_rows = []
    for row_tap in range(3):
        weight_cols = []
        for col_tap in range(3):
            window = padded[:, :, row_tap : row_tap + extent, col_tap : col_tap + extent]
            weight_cols.append(
                jnp.einsum("noxy,ncxy->oc", grad_full, window, preferred_element_type=jnp.float32)
            )
            spread = jnp.einsum(
                "oc,noxy->ncxy",
                weight[:, :, row_tap, col_tap],
                grad_full,
                preferred_element_type=jnp.float32,
            )
            grad_padded = grad_padded.at[
                :, :, row_tap : row_tap + extent, col_tap : col_tap + extent
            ].add(spread)
        weight_rows.append(jnp.stack(weight_cols, axis=-1))
    return (jnp.stack(weight_rows, axis=2), grad_padded)


def add_returned(grad_padded, returned):
    interior = grad_padded[:, :, 1:-1, 1:-1]
    interior = interior.at[:, :, 0, :].add(returned[:, 0])
    interior = interior.at[:, :, -1, :].add(returned[:, 1])
    interior = interior.at[:, :, :, 0].add(returned[:, 2])
    interior = interior.at[:, :, :, -1].add(returned[:, 3])
    return interior.astype(jnp.bfloat16)


def flatten_pixels(field):
    return field.reshape(field.shape[0], field.shape[1], -1)


def on_device_general(inputs, gluing, conv_weight, level_weight, cotangent):
    inputs = inputs.reshape(inputs.shape[0], inputs.shape[1], S, S)
    cotangent = cotangent.reshape(cotangent.shape[0], cotangent.shape[1], S // 2, S // 2)
    chan_width = inputs.shape[1]
    chan_first = lax.axis_index("chan") * chan_width
    tile_share = inputs.shape[0] // lax.axis_size("chan")
    tile_first = lax.axis_index("chan") * tile_share
    local_gluing = lax.dynamic_slice_in_dim(gluing, tile_first, tile_share, 0)
    picker = make_picker(local_gluing)
    whole_input, cot_full = (
        lax.all_to_all(inputs, "chan", split_axis=0, concat_axis=1, tiled=True),
        lax.all_to_all(cotangent, "chan", split_axis=0, concat_axis=1, tiled=True),
    )
    strips = edge_strips(whole_input)
    halo_cells = picker(
        jnp.zeros_like(strips),
        lax.all_gather(strips, ("tile", "chan"), axis=0, tiled=True),
        jnp.int32(0),
    )
    padded_whole = assemble(whole_input, orient(halo_cells, local_gluing))
    pre_act = conv_three(padded_whole, conv_weight)
    hidden = jax.nn.gelu(pre_act).astype(jnp.bfloat16)
    level_whole = conv_two(hidden, level_weight).astype(jnp.bfloat16)
    level = lax.all_to_all(level_whole, "chan", split_axis=1, concat_axis=0, tiled=True)
    grad_level, grad_hidden = level_grads(hidden, cot_full, level_weight)
    unused, pullback = jax.vjp(jax.nn.gelu, pre_act)
    grad_pre = pullback(grad_hidden)[0].astype(jnp.bfloat16)
    grad_conv, grad_padded = conv_grads(padded_whole, grad_pre, conv_weight)
    grad_conv, grad_level = lax.psum((grad_conv, grad_level), ("tile", "chan"))
    grad_conv = lax.dynamic_slice_in_dim(grad_conv, chan_first, chan_width, 1)
    grad_level = lax.dynamic_slice_in_dim(grad_level, chan_first, chan_width, 1)
    rims = border_strips(grad_padded).astype(jnp.bfloat16)
    returned = picker(
        jnp.zeros_like(rims),
        lax.all_gather(rims, ("tile", "chan"), axis=0, tiled=True),
        jnp.int32(0),
    )
    returned = orient(returned, local_gluing).astype(jnp.float32)
    grad_whole = add_returned(grad_padded, returned)
    grad_inputs = lax.all_to_all(grad_whole, "chan", split_axis=1, concat_axis=0, tiled=True)
    return (flatten_pixels(level), flatten_pixels(grad_inputs), grad_conv, grad_level)


MESH = pl.DeviceIdType.MESH
F32 = jnp.float32
BF16 = jnp.bfloat16
PIX = 1024
HALF = 32
ROOT = 0.7978845608028654
CUBIC = 0.044715


def dot(left, right):
    return jnp.dot(left, right, preferred_element_type=F32)


def dot_last(left, right):
    return lax.dot_general(left, right, (((1,), (1,)), ((), ())), preferred_element_type=F32)


def reverse_matrix():
    row = lax.broadcasted_iota(jnp.int32, (128, 128), 0)
    col = lax.broadcasted_iota(jnp.int32, (128, 128), 1)
    same = (row // 64) == (col // 64)
    return (same & ((row % 64) + (col % 64) == 63)).astype(F32).astype(BF16)


def route(codes, strips, source):
    strips = strips.astype(BF16)
    straight = (codes == 2 * source).astype(F32).astype(BF16)
    turned = (codes == 2 * source + 1).astype(F32).astype(BF16)
    reverse = dot(strips, reverse_matrix()).astype(BF16)
    return dot(straight, strips) + dot(turned, reverse)


def to_others(row, half, body):
    def step(index):
        j = lax.rem(row + index, 16)
        body(j * 2 + half, j, half)
        body(j * 2 + 1 - half, j, 1 - half)

    loop(1, 16, step)
    body(row * 2 + 1 - half, row, 1 - half)


def hail_all(row, half):
    barrier = pltpu.get_barrier_semaphore()
    to_others(
        row, half,
        lambda q, j, c: pl.semaphore_signal(barrier, inc=1, device_id=(j, c), device_id_type=MESH),
    )


def await_all():
    pl.semaphore_wait(pltpu.get_barrier_semaphore(), 31)


def pick(line_count, lane_count, source):
    lane = lax.broadcasted_iota(jnp.int32, (line_count, lane_count), 1)
    line = lax.broadcasted_iota(jnp.int32, (line_count, 1), 0)
    return (lane == source(line)).astype(F32).astype(BF16)


def split_source(line):
    row, col = line // 64, line % 64
    return ((row % 2) * 2 + col % 2) * 128 + (row // 2) * 32 + col // 2


def rows_source(line):
    return jnp.where(line < 32, line, jnp.where(line < 64, line + 960, -1))


def cols_source(line):
    return jnp.where(line < 64, -1, jnp.where(line < 96, (line - 64) * 32, (line - 96) * 32 + 31))


def unpack(field, out_ref):
    def source(line):
        channel = line % 64
        return ((channel % 32) // 2 * 2 + channel // 32) * 4 + line // 64

    mine = dot(pick(256, 128, source), field.astype(BF16))
    odd = lax.broadcasted_iota(jnp.int32, (256, 64), 0) % 2 == 1
    mine = jnp.where(odd, mine[:, 64:], mine[:, :64])
    for b in range(2):
        out_ref[64 * b:64 * b + 64, :] = jnp.concatenate(
            [mine[64 * k:64 * k + 64, 32 * b:32 * b + 32] for k in range(4)], axis=1
        ).astype(BF16)


def pack(rims):
    sides = jnp.concatenate(
        [
            jnp.concatenate([rims[:64, 32 * k:32 * k + 32], rims[64:, 32 * k:32 * k + 32]], axis=1)
            for k in range(4)
        ],
        axis=0,
    ).astype(BF16)

    def source(line):
        device = line // 4
        return line % 4 * 64 + (device % 2) * 32 + device // 2 * 2

    return jnp.concatenate(
        [dot(pick(128, 256, lambda line: source(line) + k), sides) for k in range(2)], axis=1
    )


def to_slabs(ref, value):
    for k in range(32):
        ref[k] = value[4 * k:4 * k + 4]


def remote(src, dst, send, recv, tile, chan):
    return pltpu.make_async_remote_copy(
        src_ref=src, dst_ref=dst, send_sem=send, recv_sem=recv,
        device_id=(tile, chan), device_id_type=MESH,
    )


def loop(first, last, body):
    def step(index, carry):
        body(index)
        return carry

    lax.fori_loop(first, last, step, 0)


def masks():
    pixel = lax.broadcasted_iota(jnp.int32, (64, PIX), 1)
    return pixel < 32, pixel >= 992, (pixel % 32) == 0, (pixel % 32) == 31


def patches(planes, rows, cols, out_ref):
    top, low, left, right = masks()
    zero = jnp.zeros((64, PIX), F32)

    def ahead(value, by):
        return pltpu.roll(value, by % PIX, 1)

    def column(a, s):
        if s in (0, 1):
            return planes[a][s]
        beside = zero if cols is None else cols[a]
        if s < 0:
            return jnp.where(left, beside, ahead(planes[a][1], 1))
        return jnp.where(right, beside, ahead(planes[a][0], -1))

    def outer(s):
        if rows is None:
            return zero
        if s in (0, 1):
            return rows[s]
        if s < 0:
            return jnp.where(left, 0.0, ahead(rows[1], 1))
        return jnp.where(right, 0.0, ahead(rows[0], -1))

    for s in range(-1, 3):
        even, odd = column(0, s), column(1, s)
        edge = outer(s)
        parts = (
            jnp.where(top, edge, ahead(odd, 32)), even, odd, jnp.where(low, edge, ahead(even, -32))
        )
        for r in range(4):
            first = (r * 4 + s + 1) * 64
            out_ref[first:first + 64, :] = parts[r].astype(BF16)


def whole_kernel(
    x_any, cot_any, codes_ref, taps_any, lw_any, lwt_any,
    lo_ref, out_ref, sums_ref,
    x_ref, px_ref, xo_ref, co_ref, taps_ref, lw_ref, lwt_ref, split_ref, rows_ref, cols_ref,
    strips_ref, held, all_ref, routed, arrived, halo_ref,
    z_ref, zg_ref, wide_ref, back_ref, turn_ref, level_ref, gi_ref, grads_ref,
    rims_ref, rim_held, rim_routed, rim_arrived, back, gx_ref, go_ref, bx_ref, bo_ref, near, owned, far, total,
    in_sem, big_send, big_recv, code_send, code_recv, one_send, one_recv, two_send, two_recv,
    three_send, three_recv, four_send, four_recv,
    a_send, a_recv, b_send, b_recv, c_send, c_recv, d_send, d_recv, e_send, e_recv,
):
    row, half = lax.axis_index("tile"), lax.axis_index("chan")
    me = row * 2 + half
    other = 1 - half
    core, chip = lax.rem(row, 2), row // 2
    mate = row + 1 - 2 * core
    hail_all(row, half)
    loads = [
        pltpu.make_async_copy(src, dst, in_sem.at[k])
        for k, (src, dst) in enumerate(
            (
                (x_any, x_ref),
                (taps_any, taps_ref), (lw_any, lw_ref), (lwt_any, lwt_ref),
                (cot_any.at[half], co_ref.at[half]),
            )
        )
    ]
    for load in loads:
        load.start()

    split_ref[...] = pick(512, 512, split_source)
    rows_ref[...] = pick(128, PIX, rows_source)
    cols_ref[...] = pick(128, PIX, cols_source)

    def send_all(src, dst, send, recv):
        to_others(row, half, lambda q, j, c: remote(src.at[q], dst.at[me], send, recv, j, c).start())
        dst[me] = src[me]
        return remote(src.at[pl.ds(0, 31)], dst.at[pl.ds(0, 31)], send, recv, row, other)

    def send_chips(pick_src, dst, send, recv):
        def step(index):
            j = lax.rem(chip + index, 8)
            remote(pick_src(j), dst.at[chip], send, recv, j * 2 + core, half).start()

        loop(1, 8, step)
        return remote(dst.at[pl.ds(0, 7)], dst.at[pl.ds(0, 7)], send, recv, mate, half)

    for load in loads[:1]:
        load.wait()
    x = x_ref[...].reshape(64, 4096)
    stacked = jnp.concatenate([x[:, 512 * k:512 * k + 512] for k in range(8)], axis=0)
    split = dot(stacked, split_ref[...]).astype(BF16)
    planes = [
        jnp.concatenate(
            [split[64 * k:64 * k + 64, 128 * index:128 * index + 128] for k in range(8)], axis=1
        )
        for index in range(4)
    ]
    for index in range(4):
        for t in range(2):
            px_ref[t, index] = planes[index][32 * t:32 * t + 32]
    edges = [dot_last(part, rows_ref[...] + cols_ref[...]) for part in planes]
    sides = jnp.concatenate(
        [
            jnp.concatenate([edges[index][:, 32 * s:32 * s + 32] for index in pair], axis=1)
            for s, pair in enumerate(((0, 1), (2, 3), (0, 2), (1, 3)))
        ],
        axis=0,
    ).astype(BF16)

    def strip_source(line):
        return (line % 4) * 64 + ((line // 4) % 2) * 32 + (line // 8) * 2

    strips_ref[...] = jnp.concatenate(
        [dot(pick(128, 256, lambda line: strip_source(line) + k), sides) for k in range(2)], axis=1
    ).reshape(16, 8, 128)
    await_all()

    def start_strips(index):
        j = lax.rem(row + index, 16)
        remote(codes_ref, all_ref.at[row], code_send, code_recv, j, half).start()
        remote(strips_ref.at[j], held.at[row], one_send, one_recv, j, half).start()

    loop(1, 16, start_strips)
    most = pl.ds(0, 15)
    code_all = remote(all_ref.at[most], all_ref.at[most], code_send, code_recv, row, other)
    strip_all = remote(strips_ref.at[most], held.at[most], one_send, one_recv, row, other)
    x_copy = remote(px_ref.at[other], xo_ref.at[half], big_send.at[0], big_recv.at[0], row, other)
    x_copy.start()
    held[row] = strips_ref[row]
    all_ref[row] = codes_ref[...]
    xo_ref[half] = px_ref[half]
    for load in loads[1:]:
        load.wait()
    wide_ref[...] = jnp.zeros_like(wide_ref)
    back_ref[...] = jnp.zeros_like(back_ref)
    turn_ref[...] = jnp.zeros_like(turn_ref)
    one = pick(64, 64, lambda line: line)
    for i in range(3):
        for j in range(3):
            tap = taps_ref[i * 3 + j]
            turned = dot_last(one, tap).astype(BF16)
            for a in range(2):
                for b in range(2):
                    line, at = (a * 2 + b) * 64, ((a + i) * 4 + b + j) * 64
                    back_at = ((a + 2 - i) * 4 + b + 2 - j) * 64
                    wide_ref[line:line + 64, at:at + 64] = tap
                    turn_ref[at:at + 64, line:line + 64] = turned
                    back_ref[line:line + 64, back_at:back_at + 64] = turned
    strip_all.wait_recv()
    code_all.wait_recv()
    lane = lax.broadcasted_iota(jnp.int32, (128, 128), 1)
    codes = all_ref[...].reshape(128, 128)
    to_slabs(routed, route(codes, held[...].reshape(128, 128), lane))

    halo_all = send_all(routed, arrived, two_send, two_recv)
    c_copy = remote(cot_any.at[other], co_ref.at[half], big_send.at[1], big_recv.at[1], row, other)
    c_copy.start()
    halo_all.wait_recv()
    unpack(arrived[...].reshape(128, 128), halo_ref)
    halo = halo_ref[...]
    rows = dot(halo, rows_ref[...])
    cols = dot(halo, cols_ref[...])
    x_copy.wait_recv()
    parts = [
        jnp.concatenate([xo_ref[0, index], xo_ref[1, index]], axis=0).astype(F32) for index in range(4)
    ]
    patches([parts[:2], parts[2:]], [rows[:64], rows[64:]], [cols[:64], cols[64:]], z_ref)
    pre = dot(wide_ref[...], z_ref[...])
    square = pre * pre
    bent = jnp.tanh(ROOT * pre * (1.0 + CUBIC * square))
    hidden = (0.5 * pre * (1.0 + bent)).astype(BF16)
    slope = 0.5 * (1.0 + bent) + 0.5 * pre * (1.0 - bent * bent) * ROOT * (1.0 + 3.0 * CUBIC * square)
    level_ref[...] = dot(lw_ref[...], hidden).astype(BF16).reshape(2, 64, 1024)
    c_copy.wait_recv()
    l_copy = remote(level_ref.at[other], lo_ref.at[half], big_send.at[2], big_recv.at[2], row, other)
    cot = co_ref[...].reshape(128, 1024)
    grad_pre = (dot(lwt_ref[...], cot) * slope).astype(BF16)

    edge = dot_last(grad_pre, rows_ref[...] + cols_ref[...]).astype(BF16)
    spill = dot(turn_ref[...], edge)
    small = lax.broadcasted_iota(jnp.int32, (64, 128), 1)

    def around(k):
        def block(r, s):
            first = (r * 4 + s) * 64
            return spill[first:first + 64, :]

        low = jnp.where(small < 32, block(0, k), block(3, k))
        high = jnp.where(small < 96, block(k, 0), block(k, 3))
        return jnp.where(small < 64, low, high)

    inner = small % 32
    before = jnp.where(inner == 0, 0.0, pltpu.roll(around(3), 1, 1))
    after = jnp.where(inner == 31, 0.0, pltpu.roll(around(0), 127, 1))
    to_slabs(rims_ref, pack(jnp.concatenate([around(1) + before, around(2) + after], axis=0)))

    rim_all = send_all(rims_ref, rim_held, three_send, three_recv)
    field = grad_pre.astype(F32)
    patches([[field[0:64], field[64:128]], [field[128:192], field[192:256]]], None, None, zg_ref)
    gi_ref[...] = dot(back_ref[...], zg_ref[...])
    for index in range(4):
        for h in range(2):
            first = 64 * index + 32 * h
            gx_ref[h, index] = gi_ref[first:first + 32, :].astype(BF16)
    g_copy = remote(gx_ref.at[other], go_ref.at[half], big_send.at[3], big_recv.at[3], row, other)
    g_copy.start()
    l_copy.start()
    go_ref[half] = gx_ref[half]
    lo_ref[half] = level_ref[half]

    def keep(h, first, count, lanes, value):
        for k in range(2):
            low, high = max(first, 136 * k), min(first + count, 136 * k + 136)
            if low < high:
                grads_ref[h * 2 + k, low - 136 * k:high - 136 * k, lanes] = (
                    value[low - first:high - first]
                )

    level_grad = dot_last(hidden, cot)
    for k in range(4):
        for h in range(2):
            at = 64 * k + 32 * h
            keep(h, 144 + 32 * k, 32, slice(0, 128), level_grad[at:at + 32])
    wide_grad = dot_last(z_ref[...], grad_pre)
    for i in range(3):
        for j in range(3):
            sum_tap = None
            for a in range(2):
                for b in range(2):
                    first, at = (a * 2 + b) * 64, ((a + i) * 4 + b + j) * 64
                    term = wide_grad[at:at + 64, first:first + 64]
                    sum_tap = term if sum_tap is None else sum_tap + term
            for h in range(2):
                for part in range(2):
                    at = 32 * h + 16 * part
                    keep(
                        h, 16 * (i * 3 + j), 16, slice(64 * part, 64 * part + 64), sum_tap[at:at + 16]
                    )
    near_copies = [
        remote(
            grads_ref.at[h * 2 + lax.rem(to, 2)], near.at[k], a_send.at[k], a_recv.at[k], to, h
        )
        for k, (to, h) in enumerate(((mate, half), (row, other), (mate, other)))
    ]
    for copy in near_copies:
        copy.start()

    rim_all.wait_recv()
    to_slabs(rim_routed, route(codes, rim_held[...].reshape(128, 128), lane))

    back_all = send_all(rim_routed, rim_arrived, four_send, four_recv)

    for copy in near_copies:
        copy.wait_recv()
    quarter = grads_ref[half * 2 + core]
    for k in range(3):
        quarter = quarter + near[k]
    for k in range(5):
        owned[k] = quarter[24 * k:24 * k + 24]
    owned[5, 0:16, :] = quarter[120:136]
    owned[5, 16:24, :] = jnp.zeros((8, 128), F32)
    owned[6] = jnp.zeros((24, 128), F32)
    owned[7] = jnp.zeros((24, 128), F32)

    part_all = send_chips(lambda j: owned.at[j], far, b_send, b_recv)
    far[chip] = owned[chip]

    back_all.wait_recv()
    unpack(rim_arrived[...].reshape(128, 128), back)
    rows = dot(back[...], rows_ref[...])
    cols = dot(back[...], cols_ref[...])
    top, low, left, right = masks()
    planes = []
    for a in range(2):
        for b in range(2):
            first = (a * 2 + b) * 64
            field = gi_ref[first:first + 64, :]
            field = field + jnp.where(low if a else top, rows[b * 64:b * 64 + 64], 0.0)
            field = field + jnp.where(right if b else left, cols[a * 64:a * 64 + 64], 0.0)
            rim = dot_last(field.astype(BF16), rows_ref[...] + cols_ref[...]).astype(BF16)
            for h in range(2):
                bx_ref[h, a * 2 + b] = rim[32 * h:32 * h + 32]
    e_copy = remote(bx_ref.at[other], bo_ref.at[half], e_send, e_recv, row, other)
    e_copy.start()
    bo_ref[half] = bx_ref[half]
    g_copy.wait_recv()
    e_copy.wait_recv()
    planes = []
    for a in range(2):
        for b in range(2):
            index = a * 2 + b
            rim = jnp.concatenate([bo_ref[0, index], bo_ref[1, index]], axis=0)
            field = jnp.concatenate([go_ref[0, index], go_ref[1, index]], axis=0).astype(F32)
            field = jnp.where(right if b else left, dot(rim, cols_ref[...]), field)
            field = jnp.where(low if a else top, dot(rim, rows_ref[...]), field)
            planes.append(field.astype(BF16))
    stacked = jnp.concatenate(
        [
            jnp.concatenate([part[:, 128 * k:128 * k + 128] for part in planes], axis=1)
            for k in range(8)
        ],
        axis=0,
    )
    joined = dot_last(stacked, split_ref[...]).astype(BF16)
    for k in range(8):
        for t in range(2):
            first = 64 * k + 32 * t
            out_ref[t, :, 512 * k:512 * k + 512] = joined[first:first + 32, :]

    part_all.wait_recv()
    total[...] = jnp.sum(far[...], axis=0)

    sum_all = send_chips(lambda j: total, sums_ref.at[core], c_send, c_recv)
    sums_ref[core, chip] = total[...]
    sum_all.wait_recv()
    d_copy = remote(sums_ref.at[core], sums_ref.at[core], d_send, d_recv, mate, half)
    d_copy.start()

    for copies in (code_all, strip_all, halo_all, rim_all, back_all, part_all, sum_all):
        copies.wait_send()
    for copy in near_copies:
        copy.wait_send()
    x_copy.wait_send()
    c_copy.wait_send()
    l_copy.wait()
    d_copy.wait()
    g_copy.wait_send()
    e_copy.wait_send()


def vmem(count):
    return [pl.BlockSpec(memory_space=pltpu.VMEM)] * count


def shape(dims, kind):
    return jax.ShapeDtypeStruct(dims, kind)


def params(mib, **extra):
    return pltpu.CompilerParams(vmem_limit_bytes=mib * 1024 * 1024, **extra)


def on_device_fast(inputs, gluing, conv_weight, level_weight, cotangent):
    dma = pltpu.SemaphoreType.DMA
    taps = conv_weight.transpose(2, 3, 0, 1).reshape(9, 64, 64)
    lwt = level_weight.transpose(2, 3, 1, 0).reshape(256, 128)
    codes = ((gluing[:, :, 0] * 4 + gluing[:, :, 1]) * 2 + gluing[:, :, 2]).reshape(8, 1)
    codes = jnp.broadcast_to(codes, (8, 128))
    hbm = pl.BlockSpec(memory_space=pltpu.HBM)
    eights, fours = (16, 8, 128), (32, 4, 128)
    level, grad_inputs, sums = pl.pallas_call(
        whole_kernel,
        out_shape=(
            shape((2, 64, 1024), BF16), shape((2, 32, 4096), BF16), shape((2, 8, 24, 128), F32),
        ),
        in_specs=[hbm, hbm] + vmem(1) + [hbm] * 3,
        out_specs=tuple(vmem(3)),
        scratch_shapes=[
            pltpu.VMEM(dims, kind)
            for dims, kind in (
                ((2, 32, 4096), BF16), ((2, 4, 32, 1024), BF16), ((2, 4, 32, 1024), BF16),
                ((2, 64, 1024), BF16), ((9, 64, 64), BF16), ((128, 256), BF16), ((256, 128), BF16),
                ((512, 512), BF16), ((128, 1024), BF16), ((128, 1024), BF16),
                (eights, F32), (eights, F32), (eights, jnp.int32), (fours, F32), (fours, F32),
                ((128, 128), BF16),
                ((1024, 1024), BF16), ((1024, 1024), BF16), ((256, 1024), BF16), ((256, 1024), BF16),
                ((1024, 256), BF16), ((2, 64, 1024), BF16), ((256, 1024), F32), ((4, 136, 128), F32),
                (fours, F32), (fours, F32), (fours, F32), (fours, F32), ((128, 128), BF16),
                ((2, 4, 32, 1024), BF16), ((2, 4, 32, 1024), BF16), ((2, 4, 32, 128), BF16),
                ((2, 4, 32, 128), BF16), ((3, 136, 128), F32),
                ((8, 24, 128), F32), ((8, 24, 128), F32), ((24, 128), F32),
            )
        ]
        + [
            dma((count,)) if count else dma(())
            for count in (5, 4, 4, 0, 0, 0, 0, 0, 0, 0, 0, 0, 0, 3, 3, 0, 0, 0, 0, 0, 0, 0, 0)
        ],
        compiler_params=params(53, collective_id=0, has_side_effects=True),
        name="whole",
    )(
        inputs, cotangent, codes, taps, lwt.T, lwt,
    )
    sums = sums.reshape(2, 192, 128)[:, :136].reshape(272, 128)
    grad_conv = sums[:144].reshape(3, 3, 16, 2, 64).transpose(4, 3, 2, 0, 1).reshape(64, 32, 3, 3)
    grad_level = sums[144:].reshape(2, 2, 32, 128).transpose(3, 2, 0, 1)
    return level, grad_inputs, grad_conv, grad_level


def solution(mesh):
    fits = mesh.shape["tile"] == 16 and mesh.shape["chan"] == 2
    return jax.shard_map(
        on_device_fast if fits else on_device_general,
        mesh=mesh,
        in_specs=(
            P("tile", "chan", None),
            P("tile", None, None),
            P(),
            P(),
            P("tile", "chan", None),
        ),
        out_specs=(
            P("tile", "chan", None),
            P("tile", "chan", None),
            P(None, "chan", None, None),
            P(None, "chan", None, None),
        ),
        check_vma=False,
    )
```
